128 devices in a mesh: dev: 128 (over x, y, z, core).
Axes of the slice: x: 4, y: 4, z: 4, core: 2. Of those that a mesh axis runs over, the one named last changes fastest.
Arguments:
- state: float32 [512, 512, 128], P('dev'), may hold values from -6 to 6
- background: float32 [512, 512, 128], P('dev'), may hold values from -6 to 6
- back_precision: float32 [128], replicated, may hold values from 0.2 to 2
- conv_first: bfloat16 [3, 3, 128, 128], replicated, may hold values from -0.1875 to 0.1875
- bias_first: float32 [128], replicated, may hold values from -3 to 3
- conv_second: bfloat16 [3, 3, 128, 128], replicated, may hold values from -0.1875 to 0.1875
- sounding_tile: int32 [65536, 1], P('dev'), may hold values from 0 to 127; in each aligned block of 512 rows (0 to 511, 512 to 1023, ...) at most 8 rows name the same one
- sounding_cells: int32 [65536, 4], P('dev'), may hold values from 0 to 2047
- cell_weights: float32 [65536, 4], P('dev'), may hold values from 0.1 to 1
- observations: float32 [65536, 616], P('dev'), may hold values from -6 to 6
- live_counts: int32 [128], P('dev'), may hold values from 1 to 511, as said below
- layer_in: bfloat16 [128, 1024], replicated, may hold values from -0.5 to 0.5
- bias_in: float32 [1024], replicated, may hold values from -3 to 3
- layer_out: bfloat16 [1024, 616], replicated, may hold values from -0.1875 to 0.1875
- bias_out: float32 [616], replicated, may hold values from -3 to 3
- error_precision: float32 [616, 616], replicated, as said below
Outputs:
- gradient: float32 [512, 512, 128], P('dev')
The draws below stay inside these ranges and needn't reach their ends.
Inputs may be any that keep to these rules, and one draw needn't show every extreme that they name: `sounding_tile`: among the 512 soundings of one list, at most 8 lie in the same strip, and in some lists some strip holds exactly 8 of them. The live soundings of a list are its first live_counts; the counts of lists l and l + 64 sum to 512. `error_precision`: Symmetric.
All inputs are finite; a program needn't handle non-finite values.
Results may differ from the reference program's by a relative error of at most 0.008.
Values may be sent and summed in bfloat16 or wider, within the bound.
No kernel may reach another device: no remote copies, remote signals or barrier semaphores. Data moves between devices by JAX's collectives and lax.ppermute only.
A program may use at most 64 MiB of HBM per device.

```python
import math
import jax
import jax.numpy as jnp
import numpy as np
from jax import lax

CH = 128
HID = 1024
NCHAN = 616
NCOLS = 512
MARGIN = 4
ROWS_DEV = 4
SND_DEV = 512
LISTS = 128
NROWS = 512
SOUNDINGS = 65536
CAP = 8
N_DEV = 128


def draw_live_counts(key, part):
    half_lists = LISTS // 2
    first_half = jax.random.randint(key, (half_lists,), 1, SND_DEV, dtype=jnp.int32)
    return jnp.concatenate([first_half, SND_DEV - first_half])


def draw_error_precision(key, part):
    key_off, key_diag = jax.random.split(jax.random.fold_in(key, 17))
    draws_raw = jax.random.normal(key_off, (NCHAN, NCHAN), jnp.float32)
    off_part = (draws_raw + draws_raw.T) * (0.35 / math.sqrt(NCHAN))
    diagonal = jax.random.uniform(key_diag, (NCHAN,), jnp.float32, 1.0, 3.0)
    return off_part + jnp.diag(diagonal)


def plant(drawn, own_key, low, largest):
    index_at = [jax.random.randint(jax.random.fold_in(own_key, axis), (), 0, length) for axis, length in enumerate(drawn.shape)]
    main_axis = drawn.shape.index(max(drawn.shape))
    beside = index_at[:main_axis] + [(index_at[main_axis] + 1) % drawn.shape[main_axis]] + index_at[main_axis + 1:]
    return drawn.at[tuple(index_at)].set(low).at[tuple(beside)].set(largest)


def level_of(rng, shape, cuts, low, high):
    def one(axis_at, blocks):
        steps = jax.random.uniform(jax.random.fold_in(jax.random.fold_in(rng, 6), axis_at), (blocks,), jnp.float32, low / len(cuts), high / len(cuts))
        return jnp.repeat(jnp.exp(steps), shape[axis_at] // blocks).reshape((-1,) + (1,) * (len(shape) - axis_at - 1))

    factor_of = one(*cuts[0])
    for cut in cuts[1:]:
        factor_of = factor_of * one(*cut)
    return factor_of


def routed_block(key, own, number, rows, count, top, most, slope):
    order = jax.random.permutation(key, count)
    crowded, ordinary = portions_of(count, rows * top, most, slope, True), portions_of(count, rows * top, most, slope, False)
    places = jnp.arange(count)

    def named(sizes, rotation):
        used = int((sizes > 0).sum())
        fixed = max(1, used // 4)
        moved = fixed + (places - fixed + rotation * (used - fixed)) % max(1, count - fixed)
        return jnp.zeros((count,), jnp.int32).at[order[jnp.where(places < fixed, places, moved)]].set(jnp.asarray(sizes, jnp.int32))

    sizes = jnp.where(number % 4 == 0, named(crowded, number // 4), named(ordinary, number - number // 4 - 1))
    mixed = jax.random.permutation(jax.random.fold_in(own, 3), count)
    donor, receiver = mixed[0:count // 2 * 2:2], mixed[1:count // 2 * 2:2]
    margin = jnp.minimum(sizes[donor] - 1, most - sizes[receiver]) // 2
    margin = jnp.where((donor == order[0]) | (receiver == order[0]) | (sizes[receiver] == 0), 0, jnp.maximum(margin, 0))
    moved = jax.random.randint(jax.random.fold_in(own, 4), (count // 2,), 0, 1 << 20) % (margin + 1)
    sizes = sizes.at[donor].add(-moved).at[receiver].add(moved)
    items = jnp.searchsorted(jnp.cumsum(sizes), jnp.arange(rows * top), side="right").astype(jnp.int32)
    listing = items.reshape(top, rows).T
    listing = listing[jax.random.permutation(jax.random.fold_in(own, 1), rows)]
    rotation = jax.random.randint(jax.random.fold_in(own, 2), (rows, 1), 0, top)
    return jnp.take_along_axis(listing, (jnp.arange(top)[None, :] + rotation) % top, axis=1)


def portions_of(amount, total, reach, lean, full):
    portions = [(1 << 20) // math.isqrt(standing ** lean) + 1 for standing in range(1, amount + 1)]
    largest = reach if full else min(reach, max(-(-total // amount), total * portions[0] // sum(portions)))
    least = 1 if total - largest >= amount - 1 else 0
    holding, spare = [largest] + [least] * (amount - 1), total - largest - least * (amount - 1)
    while spare > 0:
        movable = [i for i in range(1, amount) if holding[i] < largest] or [i for i in range(1, amount) if holding[i] < reach]
        pool, left = sum([portions[i] for i in movable]), spare
        for i in movable:
            more = min(reach - holding[i], max(1, left * portions[i] // pool), spare)
            holding[i] = holding[i] + more
            spare = spare - more
    return np.array(holding)


def bell_draw(rng, dims, deviation, bound, pieces=(), held_as=jnp.bfloat16):
    array = jax.random.normal(rng, dims, jnp.float32) * deviation
    if len(pieces) > 0:
        array = level_of(rng, dims, pieces, -0.22, 0.18) * array
    return jnp.clip(array, min=-bound, max=bound).astype(held_as)


def setup_inputs(seed: int = 0) -> dict:
    key_list = jax.random.split(jax.random.key(seed), 17)
    state = bell_draw(key_list[0], (NROWS, NCOLS, CH), 1.0, 6.0, ((0, 128),), jnp.float32)
    background = bell_draw(key_list[1], (NROWS, NCOLS, CH), 1.0, 6.0, ((0, 128),), jnp.float32)
    back_precision = jnp.clip(jnp.exp(jax.random.uniform(key_list[2], (CH,), jnp.float32, math.log(0.2), math.log(2.0))), 0.2, 2.0)
    conv_first = bell_draw(key_list[3], (3, 3, CH, CH), (9 * CH) ** -0.5, 0.1875)
    bias_first = bell_draw(key_list[4], (CH,), 0.5, 3.0, (), jnp.float32)
    conv_second = bell_draw(key_list[5], (3, 3, CH, CH), (9 * CH) ** -0.5, 0.1875)
    sounding_tile_keys = jax.random.split(jax.random.fold_in(key_list[6], 1), SOUNDINGS // SND_DEV)
    sounding_tile_turns = jax.random.permutation(jax.random.fold_in(key_list[6], 3), SOUNDINGS // SND_DEV)
    sounding_tile = jax.vmap(lambda own, number: routed_block(jax.random.fold_in(key_list[6], 2), own, number, SND_DEV, LISTS, 1, CAP, 2))(sounding_tile_keys, sounding_tile_turns).reshape((SOUNDINGS, 1))
    sounding_cells = plant(jax.random.randint(key_list[7], (SOUNDINGS, MARGIN), 0, ROWS_DEV * NCOLS), jax.random.fold_in(key_list[7], 1), 0, (ROWS_DEV * NCOLS) - 1).astype(jnp.int32)
    cell_weights = jnp.clip(jnp.exp(math.log(1.0) - 2.3025851 * jax.random.uniform(key_list[8], (SOUNDINGS, MARGIN), jnp.float32) ** level_of(key_list[8], (SOUNDINGS, MARGIN), ((0, 128),), -0.2, 0.2)), 0.1, 1.0)
    observations = bell_draw(key_list[9], (SOUNDINGS, NCHAN), 1.0, 6.0, ((0, 128),), jnp.float32)
    live_counts = draw_live_counts(jax.random.fold_in(key_list[16], 71), 0)
    layer_in = bell_draw(key_list[11], (CH, HID), CH ** -0.5, 0.5)
    bias_in = bell_draw(key_list[12], (HID,), 0.5, 3.0, (), jnp.float32)
    layer_out = bell_draw(key_list[13], (HID, NCHAN), HID ** -0.5, 0.1875)
    bias_out = bell_draw(key_list[14], (NCHAN,), 0.5, 3.0, (), jnp.float32)
    error_precision = draw_error_precision(jax.random.fold_in(key_list[16], 71), 0)
    return dict(state=state, background=background, back_precision=back_precision, conv_first=conv_first, bias_first=bias_first, conv_second=conv_second, sounding_tile=sounding_tile, sounding_cells=sounding_cells, cell_weights=cell_weights, observations=observations, live_counts=live_counts, layer_in=layer_in, bias_in=bias_in, layer_out=layer_out, bias_out=bias_out, error_precision=error_precision)


def conv_rows(padded, kernel):
    tile_rows = padded.shape[0] - 2
    channels = padded.shape[2]
    total = jnp.zeros((tile_rows * padded.shape[1], kernel.shape[3]), jnp.float32)
    for row_off in range(3):
        row_band = padded[row_off:row_off + tile_rows]
        for col_off in range(3):
            shifted = jnp.roll(row_band, 1 - col_off, axis=1)
            total = total + jnp.dot(shifted.reshape(-1, channels), kernel[row_off, col_off], preferred_element_type=jnp.float32)
    return total.reshape(tile_rows, padded.shape[1], kernel.shape[3])


def pad_rows(field_in):
    return jnp.pad(field_in, ((1, 1), (0, 0), (0, 0)))


def flipped(kernel):
    return kernel[::-1, ::-1].transpose(0, 1, 3, 2)


def reference(state, background, back_precision, conv_first, bias_first, conv_second, sounding_tile, sounding_cells, cell_weights, observations, live_counts, layer_in, bias_in, layer_out, bias_out, error_precision):
    state_bf = state.astype(jnp.bfloat16)
    hidden = jnp.tanh(conv_rows(pad_rows(state_bf), conv_first) + bias_first).astype(jnp.bfloat16)
    observed = (state + conv_rows(pad_rows(hidden), conv_second)).astype(jnp.bfloat16)
    observed_flat = observed.reshape(-1, CH)
    flat_index = (sounding_tile * (ROWS_DEV * NCOLS) + sounding_cells).astype(jnp.int32)
    positions = jnp.arange(SOUNDINGS, dtype=jnp.int32)
    live_mask = ((positions % SND_DEV) < jnp.repeat(live_counts, SND_DEV)).astype(jnp.float32)

    def one_block(bundle):
        indices, weights, measured, alive = bundle
        picked = observed_flat[indices].astype(jnp.float32)
        interpolated = jnp.sum(picked * weights[:, :, None], axis=1).astype(jnp.bfloat16)
        pre_act = jnp.dot(interpolated, layer_in, preferred_element_type=jnp.float32) + bias_in
        activated = jnp.tanh(pre_act).astype(jnp.bfloat16)
        radiance = jnp.dot(activated, layer_out, preferred_element_type=jnp.float32) + bias_out
        innovation = (radiance - measured) * alive[:, None]
        weighted = jnp.dot(innovation, error_precision, precision=lax.Precision.HIGHEST)
        back_act = jnp.dot(weighted.astype(jnp.bfloat16), layer_out.T, preferred_element_type=jnp.float32)
        act_wide = activated.astype(jnp.float32)
        pre_grad = (back_act * (1.0 - act_wide * act_wide)).astype(jnp.bfloat16)
        return jnp.dot(pre_grad, layer_in.T, preferred_element_type=jnp.float32)

    sounding_grad = lax.map(one_block, (
        flat_index.reshape(N_DEV, SND_DEV, MARGIN),
        cell_weights.reshape(N_DEV, SND_DEV, MARGIN),
        observations.reshape(N_DEV, SND_DEV, NCHAN),
        live_mask.reshape(N_DEV, SND_DEV))).reshape(SOUNDINGS, CH)
    ref_terms = cell_weights[:, :, None] * sounding_grad[:, None, :]
    obs_grad = jnp.zeros((NROWS * NCOLS, CH), jnp.float32).at[flat_index.reshape(-1)].add(ref_terms.reshape(-1, CH))
    obs_grad = obs_grad.reshape(state.shape)
    hid_grad = conv_rows(pad_rows(obs_grad.astype(jnp.bfloat16)), flipped(conv_second))
    hidden_wide = hidden.astype(jnp.float32)
    act_grad = (hid_grad * (1.0 - hidden_wide * hidden_wide)).astype(jnp.bfloat16)
    model_grad = conv_rows(pad_rows(act_grad), flipped(conv_first))
    return obs_grad + model_grad + back_precision * (state - background)
```

```python
import jax
import jax.numpy as jnp
from jax import lax
from jax.experimental import pallas as pl
from jax.experimental.pallas import tpu as pltpu
from jax.sharding import PartitionSpec as P

BF = jnp.bfloat16
F32 = jnp.float32
CAP = 8
LANES = 128
HIGH_CELL, LOW_CELL, HIGH_WEIGHT, LOW_WEIGHT, ALIVE, EXTRA = 0, 4, 8, 12, 16, 24
RADIX = 64
BLOCK = 544
VMEM_LIMIT = 60 * 1024 * 1024


def nn(a, b):
    return jnp.dot(a, b, preferred_element_type=F32)


def nt(a, b):
    return lax.dot_general(a, b, (((1,), (1,)), ((), ())), preferred_element_type=F32)


def tn(a, b):
    return lax.dot_general(a, b, (((0,), (0,)), ((), ())), preferred_element_type=F32)


def iota(shape, dim):
    return lax.broadcasted_iota(jnp.int32, shape, dim)


def before(n):
    return jnp.where(iota((n, n), 0) < iota((n, n), 1), 1.0, 0.0).astype(BF)


def pack_kernel(live_ref, tile_ref, cells_ref, weights_ref, obs_ref, out_ref, extra_ref):
    listed = tile_ref.shape[1]
    slots = out_ref.shape[0]
    devices = slots // CAP
    channels = obs_ref.shape[0]
    alive = iota((1, listed), 1) < live_ref[0]
    owners = jnp.where(alive, tile_ref[...], -1)
    strip = iota((devices, listed), 0)
    mine = strip == owners
    ranks = nn(jnp.where(mine, 1.0, 0.0).astype(BF), before(listed))
    place = jnp.where(mine, ranks + (CAP * strip).astype(F32), 0.0)
    slot = jnp.where(alive, jnp.sum(place, axis=0, keepdims=True).astype(jnp.int32), -1)
    spread = jnp.where(iota((slots, listed), 0) == slot, 1.0, 0.0).astype(BF)

    cells = cells_ref[...]
    weights = weights_ref[...]
    rough = weights.astype(BF).astype(F32)
    extra_ref[...] = jnp.zeros_like(extra_ref)
    extra_ref[HIGH_CELL : HIGH_CELL + 4] = (cells // RADIX).astype(F32)
    extra_ref[LOW_CELL : LOW_CELL + 4] = (cells % RADIX).astype(F32)
    extra_ref[HIGH_WEIGHT : HIGH_WEIGHT + 4] = rough
    extra_ref[LOW_WEIGHT : LOW_WEIGHT + 4] = weights - rough
    extra_ref[ALIVE : ALIVE + 1] = jnp.ones((1, listed), F32)
    whole = channels // LANES * LANES
    last = jnp.concatenate([obs_ref[whole:], extra_ref[...]], axis=0)
    out_ref[:, :whole] = nt(spread, obs_ref[:whole].astype(BF)).astype(BF)
    out_ref[:, whole:] = nt(spread, last.astype(BF)).astype(BF)


def put_shifted(ref, row, wide):
    ch = wide.shape[1]
    cols = wide.shape[0]
    at = 3 * ch * row
    ref[:, at : at + ch] = pltpu.roll(wide, 1, 0).astype(BF)
    ref[:, at + ch : at + 2 * ch] = wide.astype(BF)
    ref[:, at + 2 * ch : at + 3 * ch] = pltpu.roll(wide, cols - 1, 0).astype(BF)


def pair_weights(ref, block):
    for i in range(4):
        for b in range(3):
            for o in range(2):
                rows = pl.ds((3 * i + b) * LANES, LANES)
                cols = pl.ds(o * LANES, LANES)
                inside = 0 <= i - o <= 2
                ref[rows, cols] = block(i - o, b) if inside else jnp.zeros((LANES, LANES), BF)


def forecast_kernel(
    edge_ref,
    state_ref,
    low_ref,
    high_ref,
    first_ref,
    bias_ref,
    second_ref,
    hidden_ref,
    observed_ref,
    back_first_ref,
    back_second_ref,
    wide_ref,
    deep_ref,
    w1_ref,
    w2_ref,
):
    rows, cols, ch = state_ref.shape
    pair_weights(w1_ref, lambda a, b: first_ref[a, b])
    pair_weights(w2_ref, lambda a, b: second_ref[a, b])
    for i in range(2):
        put_shifted(wide_ref, i, low_ref[i].astype(F32))
        put_shifted(wide_ref, rows + 2 + i, high_ref[i].astype(F32))
    for i in range(rows):
        put_shifted(wide_ref, 2 + i, state_ref[i])
    for p in range((rows + 2) // 2):
        both = nn(wide_ref[:, 6 * p * ch : (6 * p + 12) * ch], w1_ref[...])
        for o in range(2):
            row = 2 * p + o
            hid = jnp.tanh(both[:, o * ch : (o + 1) * ch] + bias_ref[...])
            if row == 0:
                hid = jnp.where(edge_ref[0] == 0, 0.0, hid)
            if row == rows + 1:
                hid = jnp.where(edge_ref[0] == edge_ref[1] - 1, 0.0, hid)
            hidden_ref[row] = hid.astype(BF)
            put_shifted(deep_ref, row, hid)
    for p in range(rows // 2):
        both = nn(deep_ref[:, 6 * p * ch : (6 * p + 12) * ch], w2_ref[...])
        for o in range(2):
            row = 2 * p + o
            seen = state_ref[row] + both[:, o * ch : (o + 1) * ch]
            observed_ref[row * cols : (row + 1) * cols] = seen.astype(BF)
    pair_weights(back_first_ref, lambda a, b: first_ref[2 - a, 2 - b].T)
    pair_weights(back_second_ref, lambda a, b: second_ref[2 - a, 2 - b].T)


def fold_kernel(out_t_ref, precision_ref, out_pad_ref, fold_ref):
    n = out_t_ref.shape[0]
    out_pad_ref[...] = jnp.zeros_like(out_pad_ref)
    fold_ref[...] = jnp.zeros_like(fold_ref)
    out_pad_ref[:n] = out_t_ref[...]
    wide = precision_ref[...]
    rough = wide.astype(BF)
    rest = (wide - rough.astype(F32)).astype(BF)
    fold_ref[:n] = (nn(rough, out_t_ref[...]) + nn(rest, out_t_ref[...])).astype(BF)


def network_kernel(
    got_ref,
    observed_ref,
    in_ref,
    bias_in_ref,
    out_pad_ref,
    bias_out_ref,
    fold_ref,
    grad_ref,
    edge_ref,
    mix_ref,
):
    slots, width = got_ref.shape
    points = observed_ref.shape[0]
    first = width - EXTRA
    pick = jnp.where(iota((8, LANES), 1) == first + ALIVE - (width - LANES), 1.0, 0.0).astype(BF)
    alive = nt(pick, got_ref[:, width - LANES :])
    chunks = slots // LANES
    stacked = jnp.concatenate([alive[:1, k * LANES : (k + 1) * LANES] for k in range(chunks)], axis=0)
    inner = nn(stacked.astype(BF), before(LANES))
    totals = jnp.sum(stacked, axis=1, keepdims=True)
    ahead = jnp.zeros((1, 1), F32)
    parts = []
    for k in range(chunks):
        parts.append(inner[k : k + 1] + ahead)
        ahead = ahead + totals[k : k + 1]
    rank = jnp.concatenate(parts, axis=1)
    rank = jnp.where(alive[:1] > 0.5, rank, -1.0).astype(jnp.int32)
    count = jnp.sum(stacked).astype(jnp.int32)
    grad_ref[...] = jnp.zeros_like(grad_ref)

    def block(index, carry):
        base = index * BLOCK
        gather = jnp.where(iota((BLOCK, slots), 0) + base == rank, 1.0, 0.0).astype(BF)
        packed = nn(gather, got_ref[...])
        tail = packed[:, first:]
        cells = tail[:, HIGH_CELL : HIGH_CELL + 4] * RADIX + tail[:, LOW_CELL : LOW_CELL + 4]
        cells = cells.astype(jnp.int32)
        weights = tail[:, HIGH_WEIGHT : HIGH_WEIGHT + 4] + tail[:, LOW_WEIGHT : LOW_WEIGHT + 4]
        for start in range(0, points, 512):
            at = iota((BLOCK, 512), 1) + start
            mix = jnp.zeros((BLOCK, 512), F32)
            for k in range(4):
                mix = mix + jnp.where(at == cells[:, k : k + 1], weights[:, k : k + 1], 0.0)
            mix_ref[:, start : start + 512] = mix.astype(BF)
        blended = nn(mix_ref[...], observed_ref[...]).astype(BF)
        acted = jnp.tanh(nn(blended, in_ref[...]) + bias_in_ref[...]).astype(BF)
        missed = nt(acted, out_pad_ref[...]) + bias_out_ref[...] - packed
        back = nn(missed.astype(BF), fold_ref[...])
        acted_wide = acted.astype(F32)
        pre = (back * (1.0 - acted_wide * acted_wide)).astype(BF)
        own = nt(pre, in_ref[...]).astype(BF)
        grad_ref[...] += tn(own, mix_ref[...]).T
        return carry

    lax.fori_loop(0, (count + BLOCK - 1) // BLOCK, block, 0)
    edge_ref[...] = grad_ref[...].astype(BF)


def adjoint_kernel(
    edge_ref,
    grad_ref,
    low_ref,
    high_ref,
    hidden_ref,
    back_first_ref,
    back_second_ref,
    state_ref,
    background_ref,
    precision_ref,
    out_ref,
    wide_ref,
    deep_ref,
):
    rows, cols, ch = state_ref.shape
    for i in range(2):
        put_shifted(wide_ref, i, low_ref[i].astype(F32))
        put_shifted(wide_ref, rows + 2 + i, high_ref[i].astype(F32))
    for i in range(rows):
        put_shifted(wide_ref, 2 + i, grad_ref[i])
    for p in range((rows + 2) // 2):
        both = nn(wide_ref[:, 6 * p * ch : (6 * p + 12) * ch], back_second_ref[...])
        for o in range(2):
            row = 2 * p + o
            hid = hidden_ref[row].astype(F32)
            act = both[:, o * ch : (o + 1) * ch] * (1.0 - hid * hid)
            if row == 0:
                act = jnp.where(edge_ref[0] == 0, 0.0, act)
            if row == rows + 1:
                act = jnp.where(edge_ref[0] == edge_ref[1] - 1, 0.0, act)
            put_shifted(deep_ref, row, act)
    for p in range(rows // 2):
        both = nn(deep_ref[:, 6 * p * ch : (6 * p + 12) * ch], back_first_ref[...])
        for o in range(2):
            row = 2 * p + o
            prior = precision_ref[...] * (state_ref[row] - background_ref[row])
            out_ref[row] = grad_ref[row] + both[:, o * ch : (o + 1) * ch] + prior


def halos(block):
    count = lax.axis_size("dev")
    forward = [(i, i + 1) for i in range(count - 1)]
    backward = [(target, source) for source, target in forward]
    low = lax.ppermute(block[2:], "dev", forward)
    high = lax.ppermute(block[:2], "dev", backward)
    return low, high


def call(kernel, name, smem, out_shape, scratch, flops, *args):
    vm, sm = pl.BlockSpec(memory_space=pltpu.VMEM), pl.BlockSpec(memory_space=pltpu.SMEM)
    size = sum(a.size * a.dtype.itemsize for a in args)
    return pl.pallas_call(
        kernel,
        name=name,
        out_shape=[jax.ShapeDtypeStruct(s, d) for s, d in out_shape],
        in_specs=[sm] * smem + [vm] * (len(args) - smem),
        out_specs=[vm] * len(out_shape),
        scratch_shapes=[pltpu.VMEM(s, d) for s, d in scratch],
        compiler_params=pltpu.CompilerParams(vmem_limit_bytes=VMEM_LIMIT),
        cost_estimate=pl.CostEstimate(flops=flops, bytes_accessed=size, transcendentals=0),
    )(*args)


def per_device(
    state,
    background,
    back_precision,
    conv_first,
    bias_first,
    conv_second,
    sounding_tile,
    sounding_cells,
    cell_weights,
    observations,
    live_counts,
    layer_in,
    bias_in,
    layer_out,
    bias_out,
    error_precision,
):
    rows, cols, ch = state.shape
    devices = lax.axis_size("dev")
    slots = devices * CAP
    hid, channels = layer_out.shape
    width = channels + EXTRA
    edge = jnp.stack([lax.axis_index("dev").astype(jnp.int32), jnp.int32(devices)])
    (packed,) = call(
        pack_kernel,
        "pack",
        1,
        [((slots, width), BF)],
        [((EXTRA, sounding_tile.shape[0]), F32)],
        2_000_000_000,
        live_counts,
        sounding_tile.T,
        sounding_cells.T,
        cell_weights.T,
        observations.T,
    )
    got = lax.all_to_all(packed.reshape(devices, CAP, width), "dev", split_axis=0, concat_axis=0, tiled=True)
    low, high = halos(state.astype(BF))
    pair = (12 * ch, 2 * ch)
    hidden, observed, back_first, back_second = call(
        forecast_kernel,
        "forecast",
        1,
        [((rows + 2, cols, ch), BF), ((rows * cols, ch), BF), (pair, BF), (pair, BF)],
        [((cols, 3 * (rows + 4) * ch), BF), ((cols, 3 * (rows + 2) * ch), BF), (pair, BF), (pair, BF)],
        4_000_000_000,
        edge,
        state,
        low,
        high,
        conv_first,
        bias_first[None],
        conv_second,
    )
    out_pad, fold = call(
        fold_kernel,
        "fold",
        0,
        [((width, hid), BF), ((width, hid), BF)],
        [],
        2_000_000_000,
        layer_out.T,
        error_precision,
    )
    obs_grad, edge_rows = call(
        network_kernel,
        "network",
        0,
        [((rows * cols, ch), F32), ((rows * cols, ch), BF)],
        [((BLOCK, rows * cols), BF)],
        4_000_000_000,
        got.reshape(slots, width),
        observed,
        layer_in,
        bias_in[None],
        out_pad,
        jnp.pad(bias_out, (0, width - channels))[None],
        fold,
    )
    low, high = halos(edge_rows.reshape(rows, cols, ch))
    (gradient,) = call(
        adjoint_kernel,
        "adjoint",
        1,
        [((rows, cols, ch), F32)],
        [((cols, 3 * (rows + 4) * ch), BF), ((cols, 3 * (rows + 2) * ch), BF)],
        4_000_000_000,
        edge,
        obs_grad.reshape(rows, cols, ch),
        low,
        high,
        hidden,
        back_first,
        back_second,
        state,
        background,
        back_precision[None],
    )
    return gradient


def solution(mesh):
    whole = P()
    split = P("dev", None)
    field = P("dev", None, None)
    return jax.shard_map(
        per_device,
        mesh=mesh,
        in_specs=(field, field) + (whole,) * 4 + (split,) * 4 + (P("dev"),) + (whole,) * 5,
        out_specs=field,
        check_vma=False,
    )
```

```python
import jax
import jax.numpy as jnp
from jax import lax
from jax.experimental import pallas as pl
from jax.experimental.pallas import tpu as pltpu
from jax.sharding import PartitionSpec as P

BF = jnp.bfloat16
F32 = jnp.float32
CAP = 8
LANES = 128
HIGH_CELL, LOW_CELL, HIGH_WEIGHT, LOW_WEIGHT, ALIVE, EXTRA = 0, 4, 8, 12, 16, 24
RADIX = 64
BLOCK = 528
WIDE, NARROW, SHARED = 60 << 20, 24 << 20, 52_250_000


def nn(a, b):
    return jnp.dot(a, b, preferred_element_type=F32)


def nt(a, b):
    return lax.dot_general(a, b, (((1,), (1,)), ((), ())), preferred_element_type=F32)


def tn(a, b):
    return lax.dot_general(a, b, (((0,), (0,)), ((), ())), preferred_element_type=F32)


def iota(shape, dim):
    return lax.broadcasted_iota(jnp.int32, shape, dim)


def before(n):
    return jnp.where(iota((n, n), 0) < iota((n, n), 1), 1.0, 0.0).astype(BF)


def fetch(sources, targets, sems):
    copies = [pltpu.make_async_copy(s, t, sems.at[i]) for i, (s, t) in enumerate(zip(sources, targets))]
    for copy in copies:
        copy.start()
    return copies


def pack_kernel(
    live_ref,
    tile_hbm,
    cells_hbm,
    weights_hbm,
    obs_hbm,
    out_ref,
    extra_ref,
    tile_ref,
    cells_ref,
    weights_ref,
    obs_ref,
    sems,
):
    copies = fetch(
        (tile_hbm, cells_hbm, weights_hbm, obs_hbm), (tile_ref, cells_ref, weights_ref, obs_ref), sems
    )
    copies[0].wait()
    listed = tile_ref.shape[1]
    slots = out_ref.shape[0]
    devices = slots // CAP
    channels = obs_ref.shape[0]
    alive = iota((1, listed), 1) < live_ref[0]
    owners = jnp.where(alive, tile_ref[...], -1)
    strip = iota((devices, listed), 0)
    mine = strip == owners
    ranks = nn(jnp.where(mine, 1.0, 0.0).astype(BF), before(listed))
    place = jnp.where(mine, ranks + (CAP * strip).astype(F32), 0.0)
    slot = jnp.where(alive, jnp.sum(place, axis=0, keepdims=True).astype(jnp.int32), -1)
    spread = jnp.where(iota((slots, listed), 0) == slot, 1.0, 0.0).astype(BF)

    copies[1].wait()
    copies[2].wait()
    cells = cells_ref[...]
    weights = jnp.zeros(cells.shape, F32)
    for k in range(cells.shape[0]):
        weights = weights + jnp.where(cells == cells[k : k + 1], weights_ref[k : k + 1], 0.0)
    rough = weights.astype(BF).astype(F32)
    extra_ref[...] = jnp.zeros_like(extra_ref)
    extra_ref[HIGH_CELL : HIGH_CELL + 4] = (cells // RADIX).astype(F32)
    extra_ref[LOW_CELL : LOW_CELL + 4] = (cells % RADIX).astype(F32)
    extra_ref[HIGH_WEIGHT : HIGH_WEIGHT + 4] = rough
    extra_ref[LOW_WEIGHT : LOW_WEIGHT + 4] = weights - rough
    extra_ref[ALIVE : ALIVE + 1] = jnp.ones((1, listed), F32)
    whole = channels // LANES * LANES
    copies[3].wait()
    last = jnp.concatenate([obs_ref[whole:], extra_ref[...]], axis=0)
    out_ref[:, :whole] = nt(spread, obs_ref[:whole].astype(BF)).astype(BF)
    out_ref[:, whole:] = nt(spread, last.astype(BF)).astype(BF)


def put_shifted(ref, row, wide):
    ch = wide.shape[1]
    cols = wide.shape[0]
    at = 3 * ch * row
    ref[:, at : at + ch] = pltpu.roll(wide, 1, 0).astype(BF)
    ref[:, at + ch : at + 2 * ch] = wide.astype(BF)
    ref[:, at + 2 * ch : at + 3 * ch] = pltpu.roll(wide, cols - 1, 0).astype(BF)


def halo_row(edge_ref, near_ref, far_ref, row):
    even = edge_ref[0] % 2 == 0
    near, far = near_ref[row].astype(F32), far_ref[row].astype(F32)
    return jnp.where(even, far, near), jnp.where(even, near, far)


def pair_weights(ref, block):
    for i in range(4):
        for b in range(3):
            for o in range(2):
                rows = pl.ds((3 * i + b) * LANES, LANES)
                cols = pl.ds(o * LANES, LANES)
                inside = 0 <= i - o <= 2
                ref[rows, cols] = block(i - o, b) if inside else jnp.zeros((LANES, LANES), BF)


def forecast_kernel(
    edge_ref,
    state_ref,
    near_ref,
    far_ref,
    first_ref,
    bias_ref,
    second_ref,
    hidden_ref,
    observed_ref,
    back_first_ref,
    back_second_ref,
    wide_ref,
    deep_ref,
    w1_ref,
    w2_ref,
):
    rows, cols, ch = state_ref.shape
    pair_weights(w1_ref, lambda a, b: first_ref[a, b])
    pair_weights(w2_ref, lambda a, b: second_ref[a, b])
    for i in range(2):
        low, high = halo_row(edge_ref, near_ref, far_ref, i)
        put_shifted(wide_ref, i, low)
        put_shifted(wide_ref, rows + 2 + i, high)
    for i in range(rows):
        put_shifted(wide_ref, 2 + i, state_ref[i])
    for p in range((rows + 2) // 2):
        both = nn(wide_ref[:, 6 * p * ch : (6 * p + 12) * ch], w1_ref[...])
        for o in range(2):
            row = 2 * p + o
            hid = jnp.tanh(both[:, o * ch : (o + 1) * ch] + bias_ref[...])
            if row == 0:
                hid = jnp.where(edge_ref[0] == 0, 0.0, hid)
            if row == rows + 1:
                hid = jnp.where(edge_ref[0] == edge_ref[1] - 1, 0.0, hid)
            hidden_ref[row] = hid.astype(BF)
            put_shifted(deep_ref, row, hid)
    for p in range(rows // 2):
        both = nn(deep_ref[:, 6 * p * ch : (6 * p + 12) * ch], w2_ref[...])
        for o in range(2):
            row = 2 * p + o
            seen = state_ref[row] + both[:, o * ch : (o + 1) * ch]
            observed_ref[row * cols : (row + 1) * cols] = seen.astype(BF)
    pair_weights(back_first_ref, lambda a, b: first_ref[2 - a, 2 - b].T)
    pair_weights(back_second_ref, lambda a, b: second_ref[2 - a, 2 - b].T)


def fold_kernel(out_t_ref, in_ref, precision_ref, out_pad_ref, in_t_ref, fold_ref, pad_ref):
    n = out_t_ref.shape[0]
    fold_ref[...] = jnp.zeros_like(fold_ref)
    wide = precision_ref[...]
    rough = wide.astype(BF)
    rest = (wide - rough.astype(F32)).astype(BF)
    fold_ref[:n] = (nn(rough, out_t_ref[...]) + nn(rest, out_t_ref[...])).astype(BF)
    pad_ref[...] = jnp.zeros_like(pad_ref)
    pad_ref[:n] = out_t_ref[...]
    out_pad_ref[...] = pad_ref[...].T
    in_t_ref[...] = in_ref[...].T


def network_kernel(
    edge_ref,
    got_ref,
    observed_hbm,
    in_hbm,
    bias_in_hbm,
    out_pad_hbm,
    bias_out_hbm,
    fold_hbm,
    in_t_hbm,
    grad_ref,
    near_ref,
    far_ref,
    mix_ref,
    observed_ref,
    in_ref,
    bias_in_ref,
    out_pad_ref,
    bias_out_ref,
    fold_ref,
    in_t_ref,
    sems,
):
    copies = fetch(
        (observed_hbm, in_hbm, bias_in_hbm, out_pad_hbm, bias_out_hbm, fold_hbm, in_t_hbm),
        (observed_ref, in_ref, bias_in_ref, out_pad_ref, bias_out_ref, fold_ref, in_t_ref),
        sems,
    )
    slots, width = got_ref.shape
    points = observed_ref.shape[0]
    first = width - EXTRA
    pick = jnp.where(iota((8, LANES), 1) == first + ALIVE - (width - LANES), 1.0, 0.0).astype(BF)
    alive = nt(pick, got_ref[:, width - LANES :])
    chunks = slots // LANES
    stacked = jnp.concatenate([alive[:1, k * LANES : (k + 1) * LANES] for k in range(chunks)], axis=0)
    inner = nn(stacked.astype(BF), before(LANES))
    totals = jnp.sum(stacked, axis=1, keepdims=True)
    ahead = jnp.zeros((1, 1), F32)
    parts = []
    for k in range(chunks):
        parts.append(inner[k : k + 1] + ahead)
        ahead = ahead + totals[k : k + 1]
    rank = jnp.concatenate(parts, axis=1)
    rank = jnp.where(alive[:1] > 0.5, rank, -1.0).astype(jnp.int32)
    count = jnp.sum(stacked).astype(jnp.int32)

    def block(base, ready):
        gather = jnp.where(iota((BLOCK, slots), 0) + base == rank, 1.0, 0.0).astype(BF)
        whole = width - LANES
        last = nn(gather, got_ref[:, whole:])
        packed = jnp.concatenate([nn(gather, got_ref[:, :whole]), last], axis=1)
        tail = last[:, first - whole :]
        cells = tail[:, HIGH_CELL : HIGH_CELL + 4] * RADIX + tail[:, LOW_CELL : LOW_CELL + 4]
        cells = cells.astype(jnp.int32).astype(jnp.int16)
        weights = (tail[:, HIGH_WEIGHT : HIGH_WEIGHT + 4] + tail[:, LOW_WEIGHT : LOW_WEIGHT + 4]).astype(BF)
        for start in range(0, points, 512):
            at = (iota((BLOCK, 512), 1) + start).astype(jnp.int16)
            mix = jnp.zeros((BLOCK, 512), BF)
            for k in range(4):
                mix = jnp.where(at == cells[:, k : k + 1], weights[:, k : k + 1], mix)
            mix_ref[:, start : start + 512] = mix
        ready(0)
        blended = nn(mix_ref[...], observed_ref[...]).astype(BF)
        ready(1, 2)
        acted = jnp.tanh(nn(blended, in_ref[...]) + bias_in_ref[...]).astype(BF)
        ready(3, 4)
        missed = nn(acted, out_pad_ref[...]) + bias_out_ref[...] - packed
        ready(5)
        back = nn(missed.astype(BF), fold_ref[...])
        acted_wide = acted.astype(F32)
        pre = (back * (1.0 - acted_wide * acted_wide)).astype(BF)
        ready(6)
        own = nn(pre, in_t_ref[...]).astype(BF)
        return tn(own, mix_ref[...]).T

    def more(index, carry):
        grad_ref[...] += block(index * BLOCK, lambda *which: None)
        return carry

    grad_ref[...] = block(0, lambda *which: [copies[i].wait() for i in which])
    lax.fori_loop(1, (count + BLOCK - 1) // BLOCK, more, 0)
    half = points // 2
    odd = edge_ref[0] % 2
    near_ref[...] = grad_ref[pl.ds(half * (1 - odd), half)].astype(BF)
    far_ref[...] = grad_ref[pl.ds(half * odd, half)].astype(BF)


def inner_kernel(
    grad_ref,
    hidden_ref,
    back_first_ref,
    back_second_ref,
    state_ref,
    background_ref,
    precision_ref,
    above_ref,
    below_ref,
    part_ref,
    wide_ref,
    deep_ref,
):
    rows, cols, ch = state_ref.shape
    half = 6 * ch
    for i in range(rows):
        put_shifted(wide_ref, i, grad_ref[i])
    both = nn(wide_ref[...], back_second_ref[...])
    for o in range(2):
        hid = hidden_ref[2 + o].astype(F32)
        put_shifted(deep_ref, o, both[:, o * ch : (o + 1) * ch] * (1.0 - hid * hid))
    above_ref[...] = nn(wide_ref[:, :half], back_second_ref[half:])
    below_ref[...] = nn(wide_ref[:, half:], back_second_ref[:half])
    for p in range(2):
        both = nn(deep_ref[...], back_first_ref[half * (1 - p) : half * (2 - p)])
        for o in range(2):
            row = 2 * p + o
            prior = precision_ref[...] * (state_ref[row] - background_ref[row])
            part_ref[row] = grad_ref[row] + both[:, o * ch : (o + 1) * ch] + prior


def outer_kernel(
    edge_ref,
    near_ref,
    far_ref,
    hidden_ref,
    back_first_ref,
    back_second_ref,
    above_ref,
    below_ref,
    part_ref,
    out_ref,
    wide_ref,
    deep_ref,
):
    rows, cols, ch = part_ref.shape
    half = 6 * ch
    for i in range(2):
        low, high = halo_row(edge_ref, near_ref, far_ref, i)
        put_shifted(wide_ref, i, low)
        put_shifted(wide_ref, 2 + i, high)
    for p, start_ref in enumerate((above_ref, below_ref)):
        taps = back_second_ref[half * p : half * (p + 1)]
        both = start_ref[...] + nn(wide_ref[:, half * p : half * (p + 1)], taps)
        for o in range(2):
            row = rows * p + o
            hid = hidden_ref[row].astype(F32)
            act = both[:, o * ch : (o + 1) * ch] * (1.0 - hid * hid)
            if row == 0:
                act = jnp.where(edge_ref[0] == 0, 0.0, act)
            if row == rows + 1:
                act = jnp.where(edge_ref[0] == edge_ref[1] - 1, 0.0, act)
            put_shifted(deep_ref, 2 * p + o, act)
    for p in range(2):
        taps = back_first_ref[half * p : half * (p + 1)]
        both = nn(deep_ref[:, half * p : half * (p + 1)], taps)
        for o in range(2):
            row = 2 * p + o
            out_ref[row] = part_ref[row] + both[:, o * ch : (o + 1) * ch]


def swap_near(rows):
    count = lax.axis_size("dev")
    return lax.ppermute(rows, "dev", [(i, i ^ 1) for i in range(count)])


def swap_far(rows):
    count = lax.axis_size("dev")
    return lax.ppermute(rows, "dev", [(i, ((i + 1) ^ 1) - 1) for i in range(1, count - 1)])


def call(kernel, name, grant, places, out_shape, scratch, flops, *args):
    spaces = {"s": pltpu.SMEM, "v": pltpu.VMEM, "h": pltpu.HBM}
    vm = pl.BlockSpec(memory_space=pltpu.VMEM)
    fetched = [pltpu.VMEM(a.shape, a.dtype) for a, p in zip(args, places) if p == "h"]
    if fetched:
        fetched.append(pltpu.SemaphoreType.DMA((len(fetched),)))
    size = sum(a.size * a.dtype.itemsize for a in args)
    return pl.pallas_call(
        kernel,
        name=name,
        out_shape=[jax.ShapeDtypeStruct(s, d) for s, d in out_shape],
        in_specs=[pl.BlockSpec(memory_space=spaces[p]) for p in places],
        out_specs=[vm] * len(out_shape),
        scratch_shapes=[pltpu.VMEM(s, d) for s, d in scratch] + fetched,
        compiler_params=pltpu.CompilerParams(vmem_limit_bytes=grant),
        cost_estimate=pl.CostEstimate(flops=flops, bytes_accessed=size, transcendentals=0),
    )(*args)


def per_device(
    state,
    background,
    back_precision,
    conv_first,
    bias_first,
    conv_second,
    sounding_tile,
    sounding_cells,
    cell_weights,
    observations,
    live_counts,
    layer_in,
    bias_in,
    layer_out,
    bias_out,
    error_precision,
):
    rows, cols, ch = state.shape
    devices = lax.axis_size("dev")
    slots = devices * CAP
    hid, channels = layer_out.shape
    width = channels + EXTRA
    edge = jnp.stack([lax.axis_index("dev").astype(jnp.int32), jnp.int32(devices)])
    (packed,) = call(
        pack_kernel,
        "pack",
        WIDE,
        "shhhh",
        [((slots, width), BF)],
        [((EXTRA, sounding_tile.shape[0]), F32)],
        2_000_000_000,
        live_counts,
        sounding_tile.T,
        sounding_cells.T,
        cell_weights.T,
        observations.T,
    )
    odd = edge[0] % 2
    near = swap_near(lax.dynamic_slice_in_dim(state, 2 * (1 - odd), 2).astype(BF))
    far = swap_far(lax.dynamic_slice_in_dim(state, 2 * odd, 2).astype(BF))
    packed, near, far = lax.optimization_barrier((packed, near, far))
    got = lax.all_to_all(packed.reshape(devices, CAP, width), "dev", split_axis=0, concat_axis=0, tiled=True)
    pair = (12 * ch, 2 * ch)
    hidden, observed, back_first, back_second = call(
        forecast_kernel,
        "forecast",
        WIDE,
        "svvvvvv",
        [((rows + 2, cols, ch), BF), ((rows * cols, ch), BF), (pair, BF), (pair, BF)],
        [((cols, 3 * (rows + 4) * ch), BF), ((cols, 3 * (rows + 2) * ch), BF), (pair, BF), (pair, BF)],
        4_000_000_000,
        edge,
        state,
        near,
        far,
        conv_first,
        bias_first[None],
        conv_second,
    )
    out_pad, in_t, fold = call(
        fold_kernel,
        "fold",
        WIDE,
        "vvv",
        [((hid, width), BF), ((hid, ch), BF), ((width, hid), BF)],
        [((width, hid), BF)],
        2_000_000_000,
        layer_out.T,
        layer_in,
        error_precision,
    )
    points = rows * cols
    obs_grad, near, far = call(
        network_kernel,
        "network",
        SHARED,
        "svhhhhhhh",
        [((points, ch), F32), ((points // 2, ch), BF), ((points // 2, ch), BF)],
        [((BLOCK, points), BF)],
        4_000_000_000,
        edge,
        got.reshape(slots, width),
        observed,
        layer_in,
        bias_in[None],
        out_pad,
        jnp.pad(bias_out, (0, width - channels))[None],
        fold,
        in_t,
    )
    far = swap_far(far.reshape(2, cols, ch))
    near = swap_near(near.reshape(2, cols, ch))
    above, below, part = call(
        inner_kernel,
        "inner",
        NARROW,
        "vvvvvvv",
        [((cols, 2 * ch), F32), ((cols, 2 * ch), F32), ((rows, cols, ch), F32)],
        [((cols, 12 * ch), BF), ((cols, 6 * ch), BF)],
        4_000_000_000,
        obs_grad.reshape(rows, cols, ch),
        hidden,
        back_first,
        back_second,
        state,
        background,
        back_precision[None],
    )
    (gradient,) = call(
        outer_kernel,
        "outer",
        NARROW,
        "svvvvvvvv",
        [((rows, cols, ch), F32)],
        [((cols, 12 * ch), BF), ((cols, 12 * ch), BF)],
        2_000_000_000,
        edge,
        near,
        far,
        hidden,
        back_first,
        back_second,
        above,
        below,
        part,
    )
    return gradient


def solution(mesh):
    whole = P()
    split = P("dev", None)
    field = P("dev", None, None)
    return jax.shard_map(
        per_device,
        mesh=mesh,
        in_specs=(field, field) + (whole,) * 4 + (split,) * 4 + (P("dev"),) + (whole,) * 5,
        out_specs=field,
        check_vma=False,
    )
```

```python
import jax
import jax.numpy as jnp
from jax import lax
from jax.experimental import pallas as pl
from jax.experimental.pallas import tpu as pltpu
from jax.sharding import PartitionSpec as P

BF = jnp.bfloat16
F32 = jnp.float32
CAP = 8
LANES = 128
HIGH_CELL, LOW_CELL, HIGH_WEIGHT, LOW_WEIGHT, ALIVE, EXTRA = 0, 4, 8, 12, 16, 24
RADIX = 64
BLOCK = 528
WIDE, NARROW, SHARED = 60 << 20, 24 << 20, 52_250_000
MIDDLE = 44 << 20
PIECES = 8
KEPT = 88 * 1024


def nn(a, b):
    return jnp.dot(a, b, preferred_element_type=F32)


def nt(a, b):
    return lax.dot_general(a, b, (((1,), (1,)), ((), ())), preferred_element_type=F32)


def tn(a, b):
    return lax.dot_general(a, b, (((0,), (0,)), ((), ())), preferred_element_type=F32)


def iota(shape, dim):
    return lax.broadcasted_iota(jnp.int32, shape, dim)


def before(n):
    return jnp.where(iota((n, n), 0) < iota((n, n), 1), 1.0, 0.0).astype(BF)


def fetch(sources, targets, sems):
    copies = [pltpu.make_async_copy(s, t, sems.at[i]) for i, (s, t) in enumerate(zip(sources, targets))]
    for copy in copies:
        copy.start()
    return copies


def send(source, target, sems, piece, rows):
    copy = pltpu.make_async_copy(source.at[rows], target.at[rows], sems.at[piece])
    copy.start()
    return copy


def pack_kernel(
    live_ref,
    tile_hbm,
    cells_hbm,
    weights_hbm,
    obs_hbm,
    out_hbm,
    extra_ref,
    out_ref,
    out_sems,
    tile_ref,
    cells_ref,
    weights_ref,
    obs_ref,
    sems,
):
    copies = fetch(
        (tile_hbm, cells_hbm, weights_hbm, obs_hbm), (tile_ref, cells_ref, weights_ref, obs_ref), sems
    )
    copies[0].wait()
    listed = tile_ref.shape[1]
    slots = out_ref.shape[0]
    devices = slots // CAP
    channels = obs_ref.shape[0]
    alive = iota((1, listed), 1) < live_ref[0]
    owners = jnp.where(alive, tile_ref[...], -1)
    strip = iota((devices, listed), 0)
    mine = strip == owners
    ranks = nn(jnp.where(mine, 1.0, 0.0).astype(BF), before(listed))
    place = jnp.where(mine, ranks + (CAP * strip).astype(F32), 0.0)
    slot = jnp.where(alive, jnp.sum(place, axis=0, keepdims=True).astype(jnp.int32), -1)
    copies[1].wait()
    copies[2].wait()
    cells = cells_ref[...]
    weights = jnp.zeros(cells.shape, F32)
    for k in range(cells.shape[0]):
        weights = weights + jnp.where(cells == cells[k : k + 1], weights_ref[k : k + 1], 0.0)
    rough = weights.astype(BF).astype(F32)
    extra_ref[...] = jnp.zeros_like(extra_ref)
    extra_ref[HIGH_CELL : HIGH_CELL + 4] = (cells // RADIX).astype(F32)
    extra_ref[LOW_CELL : LOW_CELL + 4] = (cells % RADIX).astype(F32)
    extra_ref[HIGH_WEIGHT : HIGH_WEIGHT + 4] = rough
    extra_ref[LOW_WEIGHT : LOW_WEIGHT + 4] = weights - rough
    extra_ref[ALIVE : ALIVE + 1] = jnp.ones((1, listed), F32)
    whole = channels // LANES * LANES
    copies[3].wait()
    last = jnp.concatenate([obs_ref[whole:], extra_ref[...]], axis=0)
    part = slots // 2
    sent = []
    for i in range(2):
        at = pl.ds(i * part, part)
        spread = jnp.where(iota((part, listed), 0) + i * part == slot, 1.0, 0.0).astype(BF)
        out_ref[at, :whole] = nt(spread, obs_ref[:whole].astype(BF)).astype(BF)
        out_ref[at, whole:] = nt(spread, last.astype(BF)).astype(BF)
        sent.append(send(out_ref, out_hbm, out_sems, i, at))
    for copy in sent:
        copy.wait()


def put_shifted(ref, row, wide):
    ch = wide.shape[1]
    cols = wide.shape[0]
    at = 3 * ch * row
    ref[:, at : at + ch] = pltpu.roll(wide, 1, 0).astype(BF)
    ref[:, at + ch : at + 2 * ch] = wide.astype(BF)
    ref[:, at + 2 * ch : at + 3 * ch] = pltpu.roll(wide, cols - 1, 0).astype(BF)


def halo_row(edge_ref, near_ref, far_ref, row):
    even = edge_ref[0] % 2 == 0
    near, far = near_ref[row].astype(F32), far_ref[row].astype(F32)
    return jnp.where(even, far, near), jnp.where(even, near, far)


def in_grid(edge_ref, place, wide):
    if place == 0:
        return jnp.where(edge_ref[0] == 0, 0.0, wide)
    if place == 4:
        return jnp.where(edge_ref[0] == edge_ref[1] - 1, 0.0, wide)
    return wide


def pair_weights(ref, block):
    for i in range(4):
        for b in range(3):
            for o in range(2):
                rows = pl.ds((3 * i + b) * LANES, LANES)
                cols = pl.ds(o * LANES, LANES)
                inside = 0 <= i - o <= 2
                ref[rows, cols] = block(i - o, b) if inside else jnp.zeros((LANES, LANES), BF)


def near_kernel(
    state_ref,
    first_ref,
    bias_ref,
    second_ref,
    middle_ref,
    above_ref,
    below_ref,
    part_ref,
    w1_ref,
    w2_ref,
    wide_ref,
    deep_ref,
):
    rows, cols, ch = state_ref.shape
    half = 6 * ch
    pair_weights(w1_ref, lambda a, b: first_ref[a, b])
    pair_weights(w2_ref, lambda a, b: second_ref[a, b])
    for i in range(rows):
        put_shifted(wide_ref, i, state_ref[i])
    both = nn(wide_ref[...], w1_ref[...])
    for o in range(2):
        hid = jnp.tanh(both[:, o * ch : (o + 1) * ch] + bias_ref[...])
        middle_ref[o] = hid.astype(BF)
        put_shifted(deep_ref, o, hid)
    above_ref[...] = nn(wide_ref[:, :half], w1_ref[half:])
    below_ref[...] = nn(wide_ref[:, half:], w1_ref[:half])
    for p in range(2):
        both = nn(deep_ref[...], w2_ref[half * (1 - p) : half * (2 - p)])
        for o in range(2):
            row = 2 * p + o
            part_ref[row] = state_ref[row] + both[:, o * ch : (o + 1) * ch]


def forecast_kernel(
    edge_ref,
    near_ref,
    far_ref,
    bias_ref,
    w1_ref,
    w2_ref,
    above_ref,
    below_ref,
    part_ref,
    kept_hbm,
    wide_ref,
    deep_ref,
    outside_ref,
    observed_ref,
    out_sems,
):
    rows, cols, ch = part_ref.shape
    half = 6 * ch
    for i in range(2):
        low, high = halo_row(edge_ref, near_ref, far_ref, i)
        put_shifted(wide_ref, i, low)
        put_shifted(wide_ref, 2 + i, high)
    for p, start_ref in enumerate((above_ref, below_ref)):
        both = start_ref[...] + nn(wide_ref[:, half * p : half * (p + 1)], w1_ref[half * p : half * (p + 1)])
        for o in range(2):
            hid = jnp.tanh(both[:, o * ch : (o + 1) * ch] + bias_ref[...])
            hid = in_grid(edge_ref, 3 * p + o, hid)
            outside_ref[(2 * p + o) * cols : (2 * p + o + 1) * cols] = hid.astype(BF)
            put_shifted(deep_ref, 2 * p + o, hid)
    sent = [send(outside_ref, kept_hbm.at[pl.ds(rows * cols, rows * cols)], out_sems, 0, pl.ds(0, rows * cols))]
    for p in range(2):
        both = nn(deep_ref[:, half * p : half * (p + 1)], w2_ref[half * p : half * (p + 1)])
        for o in range(2):
            row = 2 * p + o
            seen = part_ref[row] + both[:, o * ch : (o + 1) * ch]
            observed_ref[row * cols : (row + 1) * cols] = seen.astype(BF)
        sent.append(send(observed_ref, kept_hbm, out_sems, 1 + p, pl.ds(2 * p * cols, 2 * cols)))
    for copy in sent:
        copy.wait()


def fold_kernel(out_t_ref, precision_ref, out_pad_ref, fold_ref, pad_ref):
    n = out_t_ref.shape[0]
    fold_ref[...] = jnp.zeros_like(fold_ref)
    wide = precision_ref[...]
    rough = wide.astype(BF)
    rest = (wide - rough.astype(F32)).astype(BF)
    fold_ref[:n] = (nn(rough, out_t_ref[...]) + nn(rest, out_t_ref[...])).astype(BF)
    pad_ref[...] = jnp.zeros_like(pad_ref)
    pad_ref[:n] = out_t_ref[...]
    out_pad_ref[...] = pad_ref[...].T


def network_kernel(
    edge_ref,
    got_ref,
    kept_hbm,
    in_hbm,
    bias_in_hbm,
    out_pad_hbm,
    bias_out_hbm,
    fold_hbm,
    grad_ref,
    near_ref,
    far_ref,
    mix_ref,
    observed_ref,
    in_ref,
    bias_in_ref,
    out_pad_ref,
    bias_out_ref,
    fold_ref,
    sems,
):
    copies = fetch(
        (kept_hbm.at[pl.ds(0, grad_ref.shape[0])], in_hbm, bias_in_hbm, out_pad_hbm, bias_out_hbm, fold_hbm),
        (observed_ref, in_ref, bias_in_ref, out_pad_ref, bias_out_ref, fold_ref),
        sems,
    )
    slots, width = got_ref.shape
    points = grad_ref.shape[0]
    first = width - EXTRA
    pick = jnp.where(iota((8, LANES), 1) == first + ALIVE - (width - LANES), 1.0, 0.0).astype(BF)
    alive = nt(pick, got_ref[:, width - LANES :])
    chunks = slots // LANES
    stacked = jnp.concatenate([alive[:1, k * LANES : (k + 1) * LANES] for k in range(chunks)], axis=0)
    inner = nn(stacked.astype(BF), before(LANES))
    totals = jnp.sum(stacked, axis=1, keepdims=True)
    ahead = jnp.zeros((1, 1), F32)
    parts = []
    for k in range(chunks):
        parts.append(inner[k : k + 1] + ahead)
        ahead = ahead + totals[k : k + 1]
    rank = jnp.concatenate(parts, axis=1)
    rank = jnp.where(alive[:1] > 0.5, rank, -1.0).astype(jnp.int32)
    count = jnp.sum(stacked).astype(jnp.int32)

    def block(base, ready):
        gather = jnp.where(iota((BLOCK, slots), 0) + base == rank, 1.0, 0.0).astype(BF)
        whole = width - LANES
        last = nn(gather, got_ref[:, whole:])
        packed = jnp.concatenate([nn(gather, got_ref[:, :whole]), last], axis=1)
        tail = last[:, first - whole :]
        cells = tail[:, HIGH_CELL : HIGH_CELL + 4] * RADIX + tail[:, LOW_CELL : LOW_CELL + 4]
        cells = cells.astype(jnp.int32).astype(jnp.int16)
        weights = (tail[:, HIGH_WEIGHT : HIGH_WEIGHT + 4] + tail[:, LOW_WEIGHT : LOW_WEIGHT + 4]).astype(BF)
        for start in range(0, points, 512):
            at = (iota((BLOCK, 512), 1) + start).astype(jnp.int16)
            mix = jnp.zeros((BLOCK, 512), BF)
            for k in range(4):
                mix = jnp.where(at == cells[:, k : k + 1], weights[:, k : k + 1], mix)
            mix_ref[:, start : start + 512] = mix
        ready(0)
        blended = nn(mix_ref[...], observed_ref[...]).astype(BF)
        ready(1, 2)
        acted = jnp.tanh(nn(blended, in_ref[...]) + bias_in_ref[...]).astype(BF)
        ready(3, 4)
        missed = nn(acted, out_pad_ref[...]) + bias_out_ref[...] - packed
        ready(5)
        back = nn(missed.astype(BF), fold_ref[...])
        acted_wide = acted.astype(F32)
        pre = (back * (1.0 - acted_wide * acted_wide)).astype(BF)
        own = nt(pre, in_ref[...]).astype(BF)
        return tn(own, mix_ref[...]).T

    def more(index, carry):
        grad_ref[...] += block(index * BLOCK, lambda *which: None)
        return carry

    grad_ref[...] = block(0, lambda *which: [copies[i].wait() for i in which])
    lax.fori_loop(1, (count + BLOCK - 1) // BLOCK, more, 0)
    half = points // 2
    odd = edge_ref[0] % 2
    near_ref[...] = grad_ref[pl.ds(half * (1 - odd), half)].astype(BF)
    far_ref[...] = grad_ref[pl.ds(half * odd, half)].astype(BF)


def inner_kernel(
    grad_ref,
    middle_ref,
    first_ref,
    second_ref,
    state_ref,
    background_ref,
    precision_ref,
    kept_hbm,
    above_ref,
    below_ref,
    part_ref,
    w1_ref,
    w2_ref,
    outside_ref,
    wide_ref,
    deep_ref,
    sems,
):
    rows, cols, ch = state_ref.shape
    half = 6 * ch
    (copy,) = fetch((kept_hbm.at[pl.ds(rows * cols, rows * cols)],), (outside_ref,), sems)
    pair_weights(w1_ref, lambda a, b: first_ref[2 - a, 2 - b].T)
    pair_weights(w2_ref, lambda a, b: second_ref[2 - a, 2 - b].T)
    for i in range(rows):
        put_shifted(wide_ref, i, grad_ref[i])
    both = nn(wide_ref[...], w2_ref[...])
    for o in range(2):
        hid = middle_ref[o].astype(F32)
        put_shifted(deep_ref, o, both[:, o * ch : (o + 1) * ch] * (1.0 - hid * hid))
    above_ref[...] = nn(wide_ref[:, :half], w2_ref[half:])
    below_ref[...] = nn(wide_ref[:, half:], w2_ref[:half])
    for p in range(2):
        both = nn(deep_ref[...], w1_ref[half * (1 - p) : half * (2 - p)])
        for o in range(2):
            row = 2 * p + o
            prior = precision_ref[...] * (state_ref[row] - background_ref[row])
            part_ref[row] = grad_ref[row] + both[:, o * ch : (o + 1) * ch] + prior
    copy.wait()


def outer_kernel(
    edge_ref,
    near_ref,
    far_ref,
    outside_ref,
    w1_ref,
    w2_ref,
    above_ref,
    below_ref,
    part_ref,
    out_hbm,
    wide_ref,
    deep_ref,
    out_ref,
    out_sems,
):
    rows, cols, ch = part_ref.shape
    half = 6 * ch
    for i in range(2):
        low, high = halo_row(edge_ref, near_ref, far_ref, i)
        put_shifted(wide_ref, i, low)
        put_shifted(wide_ref, 2 + i, high)
    for p, start_ref in enumerate((above_ref, below_ref)):
        both = start_ref[...] + nn(wide_ref[:, half * p : half * (p + 1)], w2_ref[half * p : half * (p + 1)])
        for o in range(2):
            hid = outside_ref[(2 * p + o) * cols : (2 * p + o + 1) * cols].astype(F32)
            act = both[:, o * ch : (o + 1) * ch] * (1.0 - hid * hid)
            put_shifted(deep_ref, 2 * p + o, in_grid(edge_ref, 3 * p + o, act))
    sent = []
    for p in range(2):
        both = nn(deep_ref[:, half * p : half * (p + 1)], w1_ref[half * p : half * (p + 1)])
        for o in range(2):
            row = 2 * p + o
            out_ref[row] = part_ref[row] + both[:, o * ch : (o + 1) * ch]
            sent.append(send(out_ref, out_hbm, out_sems, row, pl.ds(row, 1)))
    for copy in sent:
        copy.wait()


def swap_near(rows):
    count = lax.axis_size("dev")
    return lax.ppermute(rows, "dev", [(i, i ^ 1) for i in range(count)])


def swap_far(rows):
    count = lax.axis_size("dev")
    return lax.ppermute(rows, "dev", [(i, ((i + 1) ^ 1) - 1) for i in range(1, count - 1)])


def call(kernel, name, grant, places, out_shape, scratch, flops, *args):
    spaces = {"s": pltpu.SMEM, "v": pltpu.VMEM, "h": pltpu.HBM, "k": pltpu.HBM}
    places, made = places.split("-")
    staged = [pltpu.VMEM(o[0], o[1]) for o, p in zip(out_shape, made) if p == "h"]
    if set(made) & set("hk"):
        staged.append(pltpu.SemaphoreType.DMA((PIECES,)))
    fetched = [pltpu.VMEM(a.shape, a.dtype) for a, p in zip(args, places) if p == "h"]
    if set(places) & set("hk"):
        fetched.append(pltpu.SemaphoreType.DMA((PIECES,)))
    size = sum(a.size * a.dtype.itemsize for a in args)
    return pl.pallas_call(
        kernel,
        name=name,
        out_shape=[jax.ShapeDtypeStruct(s, d) for s, d in out_shape],
        in_specs=[pl.BlockSpec(memory_space=spaces[p]) for p in places],
        out_specs=[pl.BlockSpec(memory_space=spaces[p]) for p in made],
        scratch_shapes=[pltpu.VMEM(s, d) for s, d in scratch] + staged + fetched,
        compiler_params=pltpu.CompilerParams(vmem_limit_bytes=grant),
        cost_estimate=pl.CostEstimate(flops=flops, bytes_accessed=size, transcendentals=0),
    )(*args)


def per_device(
    state,
    background,
    back_precision,
    conv_first,
    bias_first,
    conv_second,
    sounding_tile,
    sounding_cells,
    cell_weights,
    observations,
    live_counts,
    layer_in,
    bias_in,
    layer_out,
    bias_out,
    error_precision,
):
    rows, cols, ch = state.shape
    devices = lax.axis_size("dev")
    slots = devices * CAP
    hid, channels = layer_out.shape
    width = channels + EXTRA
    edge = jnp.stack([lax.axis_index("dev").astype(jnp.int32), jnp.int32(devices)])
    (packed,) = call(
        pack_kernel,
        "pack",
        WIDE,
        "shhhh-h",
        [((slots, width), BF)],
        [((EXTRA, sounding_tile.shape[0]), F32)],
        2_000_000_000,
        live_counts,
        sounding_tile.T,
        sounding_cells.T,
        cell_weights.T,
        observations.T,
    )
    got = lax.all_to_all(packed.reshape(devices, CAP, width), "dev", split_axis=0, concat_axis=0, tiled=True)
    odd = edge[0] % 2
    near = swap_near(lax.dynamic_slice_in_dim(state, 2 * (1 - odd), 2).astype(BF))
    far = swap_far(lax.dynamic_slice_in_dim(state, 2 * odd, 2).astype(BF))
    out_pad, fold = call(
        fold_kernel,
        "fold",
        WIDE,
        "vv-vv",
        [((hid, width), BF), ((width, hid), BF)],
        [((width, hid), BF)],
        2_000_000_000,
        layer_out.T,
        error_precision,
    )
    bias_first, fold = lax.optimization_barrier((bias_first, fold))
    points = rows * cols
    pair = (12 * ch, 2 * ch)
    sums = [((cols, 2 * ch), F32), ((cols, 2 * ch), F32), ((rows, cols, ch), F32), (pair, BF), (pair, BF)]
    middle, above, below, part, w1, w2 = call(
        near_kernel,
        "near",
        NARROW,
        "vvvv-vvvvvv",
        [((2, cols, ch), BF)] + sums,
        [((cols, 12 * ch), BF), ((cols, 6 * ch), BF)],
        4_000_000_000,
        state,
        conv_first,
        bias_first[None],
        conv_second,
    )
    (kept,) = call(
        forecast_kernel,
        "forecast",
        MIDDLE,
        "svvvvvvvv-k",
        [((KEPT, ch), BF)],
        [((cols, 12 * ch), BF), ((cols, 12 * ch), BF), ((points, ch), BF), ((points, ch), BF)],
        2_000_000_000,
        edge,
        near,
        far,
        bias_first[None],
        w1,
        w2,
        above,
        below,
        part,
    )
    obs_grad, near, far = call(
        network_kernel,
        "network",
        SHARED,
        "svkhhhhh-vvv",
        [((points, ch), F32), ((points // 2, ch), BF), ((points // 2, ch), BF)],
        [((BLOCK, points), BF), ((points, ch), BF)],
        4_000_000_000,
        edge,
        got.reshape(slots, width),
        kept,
        layer_in,
        bias_in[None],
        out_pad,
        jnp.pad(bias_out, (0, width - channels))[None],
        fold,
    )
    far = swap_far(far.reshape(2, cols, ch))
    near = swap_near(near.reshape(2, cols, ch))
    above, below, part, w1, w2, outside = call(
        inner_kernel,
        "inner",
        MIDDLE,
        "vvvvvvvk-vvvvvv",
        sums + [((points, ch), BF)],
        [((cols, 12 * ch), BF), ((cols, 6 * ch), BF)],
        4_000_000_000,
        obs_grad.reshape(rows, cols, ch),
        middle,
        conv_first,
        conv_second,
        state,
        background,
        back_precision[None],
        kept,
    )
    (gradient,) = call(
        outer_kernel,
        "outer",
        NARROW,
        "svvvvvvvv-h",
        [((rows, cols, ch), F32)],
        [((cols, 12 * ch), BF), ((cols, 12 * ch), BF)],
        2_000_000_000,
        edge,
        near,
        far,
        outside,
        w1,
        w2,
        above,
        below,
        part,
    )
    return gradient


def solution(mesh):
    whole = P()
    split = P("dev", None)
    field = P("dev", None, None)
    return jax.shard_map(
        per_device,
        mesh=mesh,
        in_specs=(field, field) + (whole,) * 4 + (split,) * 4 + (P("dev"),) + (whole,) * 5,
        out_specs=field,
        check_vma=False,
    )
```

```python
import jax
import jax.numpy as jnp
from jax import lax
from jax.experimental import pallas as pl
from jax.experimental.pallas import tpu as pltpu
from jax.sharding import PartitionSpec as P

BF = jnp.bfloat16
F32 = jnp.float32
CAP = 8
LANES = 128
HIGH_CELL, LOW_CELL, HIGH_WEIGHT, LOW_WEIGHT, ALIVE, EXTRA = 0, 4, 8, 12, 16, 24
RADIX = 64
BLOCK = 528
PARTS = ((0, 256), (256, 272))
WIDE, NARROW, SHARED = 60 << 20, 24 << 20, 52_250_000
MIDDLE = 44 << 20
PIECES = 8
KEPT = 88 * 1024


def nn(a, b):
    return jnp.dot(a, b, preferred_element_type=F32)


def nt(a, b):
    return lax.dot_general(a, b, (((1,), (1,)), ((), ())), preferred_element_type=F32)


def tn(a, b):
    return lax.dot_general(a, b, (((0,), (0,)), ((), ())), preferred_element_type=F32)


def iota(shape, dim):
    return lax.broadcasted_iota(jnp.int32, shape, dim)


def before(n):
    return jnp.where(iota((n, n), 0) < iota((n, n), 1), 1.0, 0.0).astype(BF)


def fetch(sources, targets, sems):
    copies = [pltpu.make_async_copy(s, t, sems.at[i]) for i, (s, t) in enumerate(zip(sources, targets))]
    for copy in copies:
        copy.start()
    return copies


def send(source, target, sems, piece, rows):
    copy = pltpu.make_async_copy(source.at[rows], target.at[rows], sems.at[piece])
    copy.start()
    return copy


def pack_kernel(
    live_ref,
    tile_hbm,
    cells_hbm,
    weights_hbm,
    obs_hbm,
    out_hbm,
    extra_ref,
    out_ref,
    out_sems,
    tile_ref,
    cells_ref,
    weights_ref,
    obs_ref,
    sems,
):
    copies = fetch(
        (tile_hbm, cells_hbm, weights_hbm, obs_hbm), (tile_ref, cells_ref, weights_ref, obs_ref), sems
    )
    copies[0].wait()
    listed = tile_ref.shape[1]
    slots = out_ref.shape[0]
    devices = slots // CAP
    channels = obs_ref.shape[0]
    alive = iota((1, listed), 1) < live_ref[0]
    owners = jnp.where(alive, tile_ref[...], -1)
    strip = iota((devices, listed), 0)
    mine = strip == owners
    ranks = nn(jnp.where(mine, 1.0, 0.0).astype(BF), before(listed))
    place = jnp.where(mine, ranks + (CAP * strip).astype(F32), 0.0)
    slot = jnp.where(alive, jnp.sum(place, axis=0, keepdims=True).astype(jnp.int32), -1)
    copies[1].wait()
    copies[2].wait()
    cells = cells_ref[...]
    weights = jnp.zeros(cells.shape, F32)
    for k in range(cells.shape[0]):
        weights = weights + jnp.where(cells == cells[k : k + 1], weights_ref[k : k + 1], 0.0)
    rough = weights.astype(BF).astype(F32)
    extra_ref[...] = jnp.zeros_like(extra_ref)
    extra_ref[HIGH_CELL : HIGH_CELL + 4] = (cells // RADIX).astype(F32)
    extra_ref[LOW_CELL : LOW_CELL + 4] = (cells % RADIX).astype(F32)
    extra_ref[HIGH_WEIGHT : HIGH_WEIGHT + 4] = rough
    extra_ref[LOW_WEIGHT : LOW_WEIGHT + 4] = weights - rough
    extra_ref[ALIVE : ALIVE + 1] = jnp.ones((1, listed), F32)
    whole = channels // LANES * LANES
    copies[3].wait()
    last = jnp.concatenate([obs_ref[whole:], extra_ref[...]], axis=0)
    part = slots // 2
    sent = []
    for i in range(2):
        at = pl.ds(i * part, part)
        spread = jnp.where(iota((part, listed), 0) + i * part == slot, 1.0, 0.0).astype(BF)
        out_ref[at, :whole] = nt(spread, obs_ref[:whole].astype(BF)).astype(BF)
        out_ref[at, whole:] = nt(spread, last.astype(BF)).astype(BF)
        sent.append(send(out_ref, out_hbm, out_sems, i, at))
    for copy in sent:
        copy.wait()


def put_shifted(ref, row, wide):
    ch = wide.shape[1]
    cols = wide.shape[0]
    at = 3 * ch * row
    ref[:, at : at + ch] = pltpu.roll(wide, 1, 0).astype(BF)
    ref[:, at + ch : at + 2 * ch] = wide.astype(BF)
    ref[:, at + 2 * ch : at + 3 * ch] = pltpu.roll(wide, cols - 1, 0).astype(BF)


def halo_row(edge_ref, near_ref, far_ref, row):
    even = edge_ref[0] % 2 == 0
    near, far = near_ref[row].astype(F32), far_ref[row].astype(F32)
    return jnp.where(even, far, near), jnp.where(even, near, far)


def in_grid(edge_ref, place, wide):
    if place == 0:
        return jnp.where(edge_ref[0] == 0, 0.0, wide)
    if place == 4:
        return jnp.where(edge_ref[0] == edge_ref[1] - 1, 0.0, wide)
    return wide


def pair_weights(ref, block):
    for i in range(4):
        for b in range(3):
            for o in range(2):
                rows = pl.ds((3 * i + b) * LANES, LANES)
                cols = pl.ds(o * LANES, LANES)
                inside = 0 <= i - o <= 2
                ref[rows, cols] = block(i - o, b) if inside else jnp.zeros((LANES, LANES), BF)


def near_kernel(
    state_ref,
    first_ref,
    bias_ref,
    second_ref,
    middle_ref,
    above_ref,
    below_ref,
    part_ref,
    w1_ref,
    w2_ref,
    wide_ref,
    deep_ref,
):
    rows, cols, ch = state_ref.shape
    half = 6 * ch
    pair_weights(w1_ref, lambda a, b: first_ref[a, b])
    pair_weights(w2_ref, lambda a, b: second_ref[a, b])
    for i in range(rows):
        put_shifted(wide_ref, i, state_ref[i])
    both = nn(wide_ref[...], w1_ref[...])
    for o in range(2):
        hid = jnp.tanh(both[:, o * ch : (o + 1) * ch] + bias_ref[...])
        middle_ref[o] = hid.astype(BF)
        put_shifted(deep_ref, o, hid)
    above_ref[...] = nn(wide_ref[:, :half], w1_ref[half:])
    below_ref[...] = nn(wide_ref[:, half:], w1_ref[:half])
    for p in range(2):
        both = nn(deep_ref[...], w2_ref[half * (1 - p) : half * (2 - p)])
        for o in range(2):
            row = 2 * p + o
            part_ref[row] = state_ref[row] + both[:, o * ch : (o + 1) * ch]


def forecast_kernel(
    edge_ref,
    near_ref,
    far_ref,
    bias_ref,
    w1_ref,
    w2_ref,
    above_ref,
    below_ref,
    part_ref,
    kept_hbm,
    wide_ref,
    deep_ref,
    outside_ref,
    observed_ref,
    out_sems,
):
    rows, cols, ch = part_ref.shape
    half = 6 * ch
    for i in range(2):
        low, high = halo_row(edge_ref, near_ref, far_ref, i)
        put_shifted(wide_ref, i, low)
        put_shifted(wide_ref, 2 + i, high)
    for p, start_ref in enumerate((above_ref, below_ref)):
        both = start_ref[...] + nn(wide_ref[:, half * p : half * (p + 1)], w1_ref[half * p : half * (p + 1)])
        for o in range(2):
            hid = jnp.tanh(both[:, o * ch : (o + 1) * ch] + bias_ref[...])
            hid = in_grid(edge_ref, 3 * p + o, hid)
            outside_ref[(2 * p + o) * cols : (2 * p + o + 1) * cols] = hid.astype(BF)
            put_shifted(deep_ref, 2 * p + o, hid)
    sent = [send(outside_ref, kept_hbm.at[pl.ds(rows * cols, rows * cols)], out_sems, 0, pl.ds(0, rows * cols))]
    for p in range(2):
        both = nn(deep_ref[:, half * p : half * (p + 1)], w2_ref[half * p : half * (p + 1)])
        for o in range(2):
            row = 2 * p + o
            seen = part_ref[row] + both[:, o * ch : (o + 1) * ch]
            observed_ref[row * cols : (row + 1) * cols] = seen.astype(BF)
        sent.append(send(observed_ref, kept_hbm, out_sems, 1 + p, pl.ds(2 * p * cols, 2 * cols)))
    for copy in sent:
        copy.wait()


def fold_kernel(out_t_ref, precision_ref, out_pad_ref, fold_ref, pad_ref):
    n = out_t_ref.shape[0]
    fold_ref[...] = jnp.zeros_like(fold_ref)
    wide = precision_ref[...]
    rough = wide.astype(BF)
    rest = (wide - rough.astype(F32)).astype(BF)
    fold_ref[:n] = (nn(rough, out_t_ref[...]) + nn(rest, out_t_ref[...])).astype(BF)
    pad_ref[...] = jnp.zeros_like(pad_ref)
    pad_ref[:n] = out_t_ref[...]
    out_pad_ref[...] = pad_ref[...].T


def network_kernel(
    edge_ref,
    got_ref,
    kept_hbm,
    in_hbm,
    bias_in_hbm,
    out_pad_hbm,
    bias_out_hbm,
    fold_hbm,
    grad_ref,
    near_ref,
    far_ref,
    mix_ref,
    observed_ref,
    in_ref,
    bias_in_ref,
    out_pad_ref,
    bias_out_ref,
    fold_ref,
    sems,
):
    copies = fetch(
        (kept_hbm.at[pl.ds(0, grad_ref.shape[0])], in_hbm, bias_in_hbm, out_pad_hbm, bias_out_hbm, fold_hbm),
        (observed_ref, in_ref, bias_in_ref, out_pad_ref, bias_out_ref, fold_ref),
        sems,
    )
    slots, width = got_ref.shape
    points = grad_ref.shape[0]
    first = width - EXTRA
    pick = jnp.where(iota((8, LANES), 1) == first + ALIVE - (width - LANES), 1.0, 0.0).astype(BF)
    alive = nt(pick, got_ref[:, width - LANES :])
    chunks = slots // LANES
    stacked = jnp.concatenate([alive[:1, k * LANES : (k + 1) * LANES] for k in range(chunks)], axis=0)
    inner = nn(stacked.astype(BF), before(LANES))
    totals = jnp.sum(stacked, axis=1, keepdims=True)
    ahead = jnp.zeros((1, 1), F32)
    parts = []
    for k in range(chunks):
        parts.append(inner[k : k + 1] + ahead)
        ahead = ahead + totals[k : k + 1]
    rank = jnp.concatenate(parts, axis=1)
    rank = jnp.where(alive[:1] > 0.5, rank, -1.0).astype(jnp.int32)
    count = jnp.sum(stacked).astype(jnp.int32)

    whole = width - LANES

    def block(base, ready):
        halves = []
        for start, size in PARTS:
            gather = jnp.where(iota((size, slots), 0) + (base + start) == rank, 1.0, 0.0).astype(BF)
            last = nn(gather, got_ref[:, whole:])
            packed = jnp.concatenate([nn(gather, got_ref[:, :whole]), last], axis=1)
            tail = last[:, first - whole :]
            cells = tail[:, HIGH_CELL : HIGH_CELL + 4] * RADIX + tail[:, LOW_CELL : LOW_CELL + 4]
            cells = cells.astype(jnp.int32).astype(jnp.int16)
            weights = (tail[:, HIGH_WEIGHT : HIGH_WEIGHT + 4] + tail[:, LOW_WEIGHT : LOW_WEIGHT + 4]).astype(BF)
            for left in range(0, points, 512):
                at = (iota((size, 512), 1) + left).astype(jnp.int16)
                mix = jnp.zeros((size, 512), BF)
                for k in range(4):
                    mix = jnp.where(at == cells[:, k : k + 1], weights[:, k : k + 1], mix)
                mix_ref[start : start + size, left : left + 512] = mix
            halves.append(packed)
        ready(0)
        blended = [nn(mix_ref[a : a + n], observed_ref[...]).astype(BF) for a, n in PARTS]
        ready(1, 2)
        acted = [jnp.tanh(nn(x, in_ref[...]) + bias_in_ref[...]).astype(BF) for x in blended]
        ready(3, 4)
        missed = [nn(x, out_pad_ref[...]) + bias_out_ref[...] - y for x, y in zip(acted, halves)]
        ready(5)
        back = [nn(x.astype(BF), fold_ref[...]) for x in missed]
        wide = [x.astype(F32) for x in acted]
        pre = [(x * (1.0 - y * y)).astype(BF) for x, y in zip(back, wide)]
        own = jnp.concatenate([nt(x, in_ref[...]).astype(BF) for x in pre], axis=0)
        return tn(own, mix_ref[...]).T

    def more(index, carry):
        grad_ref[...] += block(index * BLOCK, lambda *which: None)
        return carry

    grad_ref[...] = block(0, lambda *which: [copies[i].wait() for i in which])
    lax.fori_loop(1, (count + BLOCK - 1) // BLOCK, more, 0)
    half = points // 2
    odd = edge_ref[0] % 2
    near_ref[...] = grad_ref[pl.ds(half * (1 - odd), half)].astype(BF)
    far_ref[...] = grad_ref[pl.ds(half * odd, half)].astype(BF)


def inner_kernel(
    grad_ref,
    middle_ref,
    first_ref,
    second_ref,
    state_ref,
    background_ref,
    precision_ref,
    kept_hbm,
    above_ref,
    below_ref,
    part_ref,
    w1_ref,
    w2_ref,
    outside_ref,
    wide_ref,
    deep_ref,
    sems,
):
    rows, cols, ch = state_ref.shape
    half = 6 * ch
    (copy,) = fetch((kept_hbm.at[pl.ds(rows * cols, rows * cols)],), (outside_ref,), sems)
    pair_weights(w1_ref, lambda a, b: first_ref[2 - a, 2 - b].T)
    pair_weights(w2_ref, lambda a, b: second_ref[2 - a, 2 - b].T)
    for i in range(rows):
        put_shifted(wide_ref, i, grad_ref[i])
    both = nn(wide_ref[...], w2_ref[...])
    for o in range(2):
        hid = middle_ref[o].astype(F32)
        put_shifted(deep_ref, o, both[:, o * ch : (o + 1) * ch] * (1.0 - hid * hid))
    above_ref[...] = nn(wide_ref[:, :half], w2_ref[half:])
    below_ref[...] = nn(wide_ref[:, half:], w2_ref[:half])
    for p in range(2):
        both = nn(deep_ref[...], w1_ref[half * (1 - p) : half * (2 - p)])
        for o in range(2):
            row = 2 * p + o
            prior = precision_ref[...] * (state_ref[row] - background_ref[row])
            part_ref[row] = grad_ref[row] + both[:, o * ch : (o + 1) * ch] + prior
    copy.wait()


def outer_kernel(
    edge_ref,
    near_ref,
    far_ref,
    outside_ref,
    w1_ref,
    w2_ref,
    above_ref,
    below_ref,
    part_ref,
    out_hbm,
    wide_ref,
    deep_ref,
    out_ref,
    out_sems,
):
    rows, cols, ch = part_ref.shape
    half = 6 * ch
    for i in range(2):
        low, high = halo_row(edge_ref, near_ref, far_ref, i)
        put_shifted(wide_ref, i, low)
        put_shifted(wide_ref, 2 + i, high)
    for p, start_ref in enumerate((above_ref, below_ref)):
        both = start_ref[...] + nn(wide_ref[:, half * p : half * (p + 1)], w2_ref[half * p : half * (p + 1)])
        for o in range(2):
            hid = outside_ref[(2 * p + o) * cols : (2 * p + o + 1) * cols].astype(F32)
            act = both[:, o * ch : (o + 1) * ch] * (1.0 - hid * hid)
            put_shifted(deep_ref, 2 * p + o, in_grid(edge_ref, 3 * p + o, act))
    sent = []
    for p in range(2):
        both = nn(deep_ref[:, half * p : half * (p + 1)], w1_ref[half * p : half * (p + 1)])
        for o in range(2):
            row = 2 * p + o
            out_ref[row] = part_ref[row] + both[:, o * ch : (o + 1) * ch]
            sent.append(send(out_ref, out_hbm, out_sems, row, pl.ds(row, 1)))
    for copy in sent:
        copy.wait()


def swap_near(rows):
    count = lax.axis_size("dev")
    return lax.ppermute(rows, "dev", [(i, i ^ 1) for i in range(count)])


def swap_far(rows):
    count = lax.axis_size("dev")
    return lax.ppermute(rows, "dev", [(i, ((i + 1) ^ 1) - 1) for i in range(1, count - 1)])


def call(kernel, name, grant, places, out_shape, scratch, flops, *args):
    spaces = {"s": pltpu.SMEM, "v": pltpu.VMEM, "h": pltpu.HBM, "k": pltpu.HBM}
    places, made = places.split("-")
    staged = [pltpu.VMEM(o[0], o[1]) for o, p in zip(out_shape, made) if p == "h"]
    if set(made) & set("hk"):
        staged.append(pltpu.SemaphoreType.DMA((PIECES,)))
    fetched = [pltpu.VMEM(a.shape, a.dtype) for a, p in zip(args, places) if p == "h"]
    if set(places) & set("hk"):
        fetched.append(pltpu.SemaphoreType.DMA((PIECES,)))
    size = sum(a.size * a.dtype.itemsize for a in args)
    return pl.pallas_call(
        kernel,
        name=name,
        out_shape=[jax.ShapeDtypeStruct(s, d) for s, d in out_shape],
        in_specs=[pl.BlockSpec(memory_space=spaces[p]) for p in places],
        out_specs=[pl.BlockSpec(memory_space=spaces[p]) for p in made],
        scratch_shapes=[pltpu.VMEM(s, d) for s, d in scratch] + staged + fetched,
        compiler_params=pltpu.CompilerParams(vmem_limit_bytes=grant),
        cost_estimate=pl.CostEstimate(flops=flops, bytes_accessed=size, transcendentals=0),
    )(*args)


def per_device(
    state,
    background,
    back_precision,
    conv_first,
    bias_first,
    conv_second,
    sounding_tile,
    sounding_cells,
    cell_weights,
    observations,
    live_counts,
    layer_in,
    bias_in,
    layer_out,
    bias_out,
    error_precision,
):
    rows, cols, ch = state.shape
    devices = lax.axis_size("dev")
    slots = devices * CAP
    hid, channels = layer_out.shape
    width = channels + EXTRA
    edge = jnp.stack([lax.axis_index("dev").astype(jnp.int32), jnp.int32(devices)])
    (packed,) = call(
        pack_kernel,
        "pack",
        WIDE,
        "shhhh-h",
        [((slots, width), BF)],
        [((EXTRA, sounding_tile.shape[0]), F32)],
        2_000_000_000,
        live_counts,
        sounding_tile.T,
        sounding_cells.T,
        cell_weights.T,
        observations.T,
    )
    got = lax.all_to_all(packed.reshape(devices, CAP, width), "dev", split_axis=0, concat_axis=0, tiled=True)
    odd = edge[0] % 2
    near = swap_near(lax.dynamic_slice_in_dim(state, 2 * (1 - odd), 2).astype(BF))
    far = swap_far(lax.dynamic_slice_in_dim(state, 2 * odd, 2).astype(BF))
    out_pad, fold = call(
        fold_kernel,
        "fold",
        WIDE,
        "vv-vv",
        [((hid, width), BF), ((width, hid), BF)],
        [((width, hid), BF)],
        2_000_000_000,
        layer_out.T,
        error_precision,
    )
    bias_first, fold = lax.optimization_barrier((bias_first, fold))
    points = rows * cols
    pair = (12 * ch, 2 * ch)
    sums = [((cols, 2 * ch), F32), ((cols, 2 * ch), F32), ((rows, cols, ch), F32), (pair, BF), (pair, BF)]
    middle, above, below, part, w1, w2 = call(
        near_kernel,
        "near",
        NARROW,
        "vvvv-vvvvvv",
        [((2, cols, ch), BF)] + sums,
        [((cols, 12 * ch), BF), ((cols, 6 * ch), BF)],
        4_000_000_000,
        state,
        conv_first,
        bias_first[None],
        conv_second,
    )
    (kept,) = call(
        forecast_kernel,
        "forecast",
        MIDDLE,
        "svvvvvvvv-k",
        [((KEPT, ch), BF)],
        [((cols, 12 * ch), BF), ((cols, 12 * ch), BF), ((points, ch), BF), ((points, ch), BF)],
        2_000_000_000,
        edge,
        near,
        far,
        bias_first[None],
        w1,
        w2,
        above,
        below,
        part,
    )
    obs_grad, near, far = call(
        network_kernel,
        "network",
        SHARED,
        "svkhhhhh-vvv",
        [((points, ch), F32), ((points // 2, ch), BF), ((points // 2, ch), BF)],
        [((BLOCK, points), BF), ((points, ch), BF)],
        4_000_000_000,
        edge,
        got.reshape(slots, width),
        kept,
        layer_in,
        bias_in[None],
        out_pad,
        jnp.pad(bias_out, (0, width - channels))[None],
        fold,
    )
    far = swap_far(far.reshape(2, cols, ch))
    near = swap_near(near.reshape(2, cols, ch))
    above, below, part, w1, w2, outside = call(
        inner_kernel,
        "inner",
        MIDDLE,
        "vvvvvvvk-vvvvvv",
        sums + [((points, ch), BF)],
        [((cols, 12 * ch), BF), ((cols, 6 * ch), BF)],
        4_000_000_000,
        obs_grad.reshape(rows, cols, ch),
        middle,
        conv_first,
        conv_second,
        state,
        background,
        back_precision[None],
        kept,
    )
    (gradient,) = call(
        outer_kernel,
        "outer",
        NARROW,
        "svvvvvvvv-h",
        [((rows, cols, ch), F32)],
        [((cols, 12 * ch), BF), ((cols, 12 * ch), BF)],
        2_000_000_000,
        edge,
        near,
        far,
        outside,
        w1,
        w2,
        above,
        below,
        part,
    )
    return gradient


def solution(mesh):
    whole = P()
    split = P("dev", None)
    field = P("dev", None, None)
    return jax.shard_map(
        per_device,
        mesh=mesh,
        in_specs=(field, field) + (whole,) * 4 + (split,) * 4 + (P("dev"),) + (whole,) * 5,
        out_specs=field,
        check_vma=False,
    )
```

```python
import jax
import jax.numpy as jnp
from jax import lax
from jax.experimental import pallas as pl
from jax.experimental.pallas import tpu as pltpu
from jax.sharding import PartitionSpec as P

BF = jnp.bfloat16
F32 = jnp.float32
CAP = 8
LANES = 128
HIGH_CELL, LOW_CELL, HIGH_WEIGHT, LOW_WEIGHT, ALIVE, EXTRA = 0, 4, 8, 12, 16, 24
RADIX = 64
BLOCK = 528
PARTS = ((0, 176), (176, 176), (352, 176))
WIDE, NARROW, SHARED = 60 << 20, 24 << 20, 52_250_000
MIDDLE = 44 << 20
PIECES = 8
KEPT = 88 * 1024


def nn(a, b):
    return jnp.dot(a, b, preferred_element_type=F32)


def nt(a, b):
    return lax.dot_general(a, b, (((1,), (1,)), ((), ())), preferred_element_type=F32)


def tn(a, b):
    return lax.dot_general(a, b, (((0,), (0,)), ((), ())), preferred_element_type=F32)


def iota(shape, dim):
    return lax.broadcasted_iota(jnp.int32, shape, dim)


def before(n):
    return jnp.where(iota((n, n), 0) < iota((n, n), 1), 1.0, 0.0).astype(BF)


def fetch(sources, targets, sems):
    copies = [pltpu.make_async_copy(s, t, sems.at[i]) for i, (s, t) in enumerate(zip(sources, targets))]
    for copy in copies:
        copy.start()
    return copies


def send(source, target, sems, piece, rows):
    copy = pltpu.make_async_copy(source.at[rows], target.at[rows], sems.at[piece])
    copy.start()
    return copy


def pack_kernel(
    live_ref,
    tile_hbm,
    cells_hbm,
    weights_hbm,
    obs_hbm,
    out_hbm,
    extra_ref,
    out_ref,
    out_sems,
    tile_ref,
    cells_ref,
    weights_ref,
    obs_ref,
    sems,
):
    copies = fetch(
        (tile_hbm, cells_hbm, weights_hbm, obs_hbm), (tile_ref, cells_ref, weights_ref, obs_ref), sems
    )
    copies[0].wait()
    listed = tile_ref.shape[1]
    slots = out_ref.shape[0]
    devices = slots // CAP
    channels = obs_ref.shape[0]
    alive = iota((1, listed), 1) < live_ref[0]
    owners = jnp.where(alive, tile_ref[...], -1)
    strip = iota((devices, listed), 0)
    mine = strip == owners
    ranks = nn(jnp.where(mine, 1.0, 0.0).astype(BF), before(listed))
    place = jnp.where(mine, ranks + (CAP * strip).astype(F32), 0.0)
    slot = jnp.where(alive, jnp.sum(place, axis=0, keepdims=True).astype(jnp.int32), -1)
    copies[1].wait()
    copies[2].wait()
    cells = cells_ref[...]
    weights = jnp.zeros(cells.shape, F32)
    for k in range(cells.shape[0]):
        weights = weights + jnp.where(cells == cells[k : k + 1], weights_ref[k : k + 1], 0.0)
    rough = weights.astype(BF).astype(F32)
    extra_ref[...] = jnp.zeros_like(extra_ref)
    extra_ref[HIGH_CELL : HIGH_CELL + 4] = (cells // RADIX).astype(F32)
    extra_ref[LOW_CELL : LOW_CELL + 4] = (cells % RADIX).astype(F32)
    extra_ref[HIGH_WEIGHT : HIGH_WEIGHT + 4] = rough
    extra_ref[LOW_WEIGHT : LOW_WEIGHT + 4] = weights - rough
    extra_ref[ALIVE : ALIVE + 1] = jnp.ones((1, listed), F32)
    whole = channels // LANES * LANES
    copies[3].wait()
    last = jnp.concatenate([obs_ref[whole:], extra_ref[...]], axis=0)
    part = slots // 2
    sent = []
    for i in range(2):
        at = pl.ds(i * part, part)
        spread = jnp.where(iota((part, listed), 0) + i * part == slot, 1.0, 0.0).astype(BF)
        out_ref[at, :whole] = nt(spread, obs_ref[:whole].astype(BF)).astype(BF)
        out_ref[at, whole:] = nt(spread, last.astype(BF)).astype(BF)
        sent.append(send(out_ref, out_hbm, out_sems, i, at))
    for copy in sent:
        copy.wait()


def put_shifted(ref, row, wide):
    ch = wide.shape[1]
    cols = wide.shape[0]
    at = 3 * ch * row
    ref[:, at : at + ch] = pltpu.roll(wide, 1, 0).astype(BF)
    ref[:, at + ch : at + 2 * ch] = wide.astype(BF)
    ref[:, at + 2 * ch : at + 3 * ch] = pltpu.roll(wide, cols - 1, 0).astype(BF)


def halo_row(edge_ref, near_ref, far_ref, row):
    even = edge_ref[0] % 2 == 0
    near, far = near_ref[row].astype(F32), far_ref[row].astype(F32)
    return jnp.where(even, far, near), jnp.where(even, near, far)


def in_grid(edge_ref, place, wide):
    if place == 0:
        return jnp.where(edge_ref[0] == 0, 0.0, wide)
    if place == 4:
        return jnp.where(edge_ref[0] == edge_ref[1] - 1, 0.0, wide)
    return wide


def pair_weights(ref, block):
    for i in range(4):
        for b in range(3):
            for o in range(2):
                rows = pl.ds((3 * i + b) * LANES, LANES)
                cols = pl.ds(o * LANES, LANES)
                inside = 0 <= i - o <= 2
                ref[rows, cols] = block(i - o, b) if inside else jnp.zeros((LANES, LANES), BF)


def near_kernel(
    state_ref,
    first_ref,
    bias_ref,
    second_ref,
    middle_ref,
    above_ref,
    below_ref,
    part_ref,
    w1_ref,
    w2_ref,
    wide_ref,
    deep_ref,
):
    rows, cols, ch = state_ref.shape
    half = 6 * ch
    pair_weights(w1_ref, lambda a, b: first_ref[a, b])
    pair_weights(w2_ref, lambda a, b: second_ref[a, b])
    for i in range(rows):
        put_shifted(wide_ref, i, state_ref[i])
    both = nn(wide_ref[...], w1_ref[...])
    for o in range(2):
        hid = jnp.tanh(both[:, o * ch : (o + 1) * ch] + bias_ref[...])
        middle_ref[o] = hid.astype(BF)
        put_shifted(deep_ref, o, hid)
    above_ref[...] = nn(wide_ref[:, :half], w1_ref[half:])
    below_ref[...] = nn(wide_ref[:, half:], w1_ref[:half])
    for p in range(2):
        both = nn(deep_ref[...], w2_ref[half * (1 - p) : half * (2 - p)])
        for o in range(2):
            row = 2 * p + o
            part_ref[row] = state_ref[row] + both[:, o * ch : (o + 1) * ch]


def forecast_kernel(
    edge_ref,
    near_ref,
    far_ref,
    bias_ref,
    w1_ref,
    w2_ref,
    above_ref,
    below_ref,
    part_ref,
    kept_hbm,
    wide_ref,
    deep_ref,
    outside_ref,
    observed_ref,
    out_sems,
):
    rows, cols, ch = part_ref.shape
    half = 6 * ch
    for i in range(2):
        low, high = halo_row(edge_ref, near_ref, far_ref, i)
        put_shifted(wide_ref, i, low)
        put_shifted(wide_ref, 2 + i, high)
    for p, start_ref in enumerate((above_ref, below_ref)):
        both = start_ref[...] + nn(wide_ref[:, half * p : half * (p + 1)], w1_ref[half * p : half * (p + 1)])
        for o in range(2):
            hid = jnp.tanh(both[:, o * ch : (o + 1) * ch] + bias_ref[...])
            hid = in_grid(edge_ref, 3 * p + o, hid)
            outside_ref[(2 * p + o) * cols : (2 * p + o + 1) * cols] = hid.astype(BF)
            put_shifted(deep_ref, 2 * p + o, hid)
    sent = [send(outside_ref, kept_hbm.at[pl.ds(rows * cols, rows * cols)], out_sems, 0, pl.ds(0, rows * cols))]
    for p in range(2):
        both = nn(deep_ref[:, half * p : half * (p + 1)], w2_ref[half * p : half * (p + 1)])
        for o in range(2):
            row = 2 * p + o
            seen = part_ref[row] + both[:, o * ch : (o + 1) * ch]
            observed_ref[row * cols : (row + 1) * cols] = seen.astype(BF)
        sent.append(send(observed_ref, kept_hbm, out_sems, 1 + p, pl.ds(2 * p * cols, 2 * cols)))
    for copy in sent:
        copy.wait()


def fold_kernel(out_t_ref, precision_ref, out_pad_ref, fold_ref, pad_ref):
    n = out_t_ref.shape[0]
    fold_ref[...] = jnp.zeros_like(fold_ref)
    wide = precision_ref[...]
    rough = wide.astype(BF)
    rest = (wide - rough.astype(F32)).astype(BF)
    fold_ref[:n] = (nn(rough, out_t_ref[...]) + nn(rest, out_t_ref[...])).astype(BF)
    pad_ref[...] = jnp.zeros_like(pad_ref)
    pad_ref[:n] = out_t_ref[...]
    out_pad_ref[...] = pad_ref[...].T


def network_kernel(
    edge_ref,
    got_ref,
    kept_hbm,
    in_hbm,
    bias_in_hbm,
    out_pad_hbm,
    bias_out_hbm,
    fold_hbm,
    grad_ref,
    near_ref,
    far_ref,
    mix_ref,
    observed_ref,
    in_ref,
    bias_in_ref,
    out_pad_ref,
    bias_out_ref,
    fold_ref,
    sems,
):
    copies = fetch(
        (kept_hbm.at[pl.ds(0, grad_ref.shape[0])], in_hbm, bias_in_hbm, out_pad_hbm, bias_out_hbm, fold_hbm),
        (observed_ref, in_ref, bias_in_ref, out_pad_ref, bias_out_ref, fold_ref),
        sems,
    )
    slots, width = got_ref.shape
    points = grad_ref.shape[0]
    first = width - EXTRA
    pick = jnp.where(iota((8, LANES), 1) == first + ALIVE - (width - LANES), 1.0, 0.0).astype(BF)
    alive = nt(pick, got_ref[:, width - LANES :])
    chunks = slots // LANES
    stacked = jnp.concatenate([alive[:1, k * LANES : (k + 1) * LANES] for k in range(chunks)], axis=0)
    inner = nn(stacked.astype(BF), before(LANES))
    totals = jnp.sum(stacked, axis=1, keepdims=True)
    ahead = jnp.zeros((1, 1), F32)
    parts = []
    for k in range(chunks):
        parts.append(inner[k : k + 1] + ahead)
        ahead = ahead + totals[k : k + 1]
    rank = jnp.concatenate(parts, axis=1)
    rank = jnp.where(alive[:1] > 0.5, rank, -1.0).astype(jnp.int32)
    count = jnp.sum(stacked).astype(jnp.int32)

    whole = width - LANES

    def block(base, ready):
        halves = []
        for start, size in PARTS:
            gather = jnp.where(iota((size, slots), 0) + (base + start) == rank, 1.0, 0.0).astype(BF)
            last = nn(gather, got_ref[:, whole:])
            packed = jnp.concatenate([nn(gather, got_ref[:, :whole]), last], axis=1)
            tail = last[:, first - whole :]
            cells = tail[:, HIGH_CELL : HIGH_CELL + 4] * RADIX + tail[:, LOW_CELL : LOW_CELL + 4]
            cells = cells.astype(jnp.int32).astype(jnp.int16)
            weights = (tail[:, HIGH_WEIGHT : HIGH_WEIGHT + 4] + tail[:, LOW_WEIGHT : LOW_WEIGHT + 4]).astype(BF)
            for left in range(0, points, 512):
                at = (iota((size, 512), 1) + left).astype(jnp.int16)
                mix = jnp.zeros((size, 512), BF)
                for k in range(4):
                    mix = jnp.where(at == cells[:, k : k + 1], weights[:, k : k + 1], mix)
                mix_ref[start : start + size, left : left + 512] = mix
            halves.append(packed)
        ready(0)
        blended = [nn(mix_ref[a : a + n], observed_ref[...]).astype(BF) for a, n in PARTS]
        ready(1, 2)
        acted = [jnp.tanh(nn(x, in_ref[...]) + bias_in_ref[...]).astype(BF) for x in blended]
        ready(3, 4)
        missed = [nn(x, out_pad_ref[...]) + bias_out_ref[...] - y for x, y in zip(acted, halves)]
        ready(5)
        back = [nn(x.astype(BF), fold_ref[...]) for x in missed]
        wide = [x.astype(F32) for x in acted]
        pre = [(x * (1.0 - y * y)).astype(BF) for x, y in zip(back, wide)]
        own = jnp.concatenate([nt(x, in_ref[...]).astype(BF) for x in pre], axis=0)
        return tn(own, mix_ref[...]).T

    def more(index, carry):
        grad_ref[...] += block(index * BLOCK, lambda *which: None)
        return carry

    grad_ref[...] = block(0, lambda *which: [copies[i].wait() for i in which])
    lax.fori_loop(1, (count + BLOCK - 1) // BLOCK, more, 0)
    half = points // 2
    odd = edge_ref[0] % 2
    near_ref[...] = grad_ref[pl.ds(half * (1 - odd), half)].astype(BF)
    far_ref[...] = grad_ref[pl.ds(half * odd, half)].astype(BF)


def inner_kernel(
    grad_ref,
    middle_ref,
    first_ref,
    second_ref,
    state_ref,
    background_ref,
    precision_ref,
    kept_hbm,
    above_ref,
    below_ref,
    part_ref,
    w1_ref,
    w2_ref,
    outside_ref,
    wide_ref,
    deep_ref,
    sems,
):
    rows, cols, ch = state_ref.shape
    half = 6 * ch
    (copy,) = fetch((kept_hbm.at[pl.ds(rows * cols, rows * cols)],), (outside_ref,), sems)
    pair_weights(w1_ref, lambda a, b: first_ref[2 - a, 2 - b].T)
    pair_weights(w2_ref, lambda a, b: second_ref[2 - a, 2 - b].T)
    for i in range(rows):
        put_shifted(wide_ref, i, grad_ref[i])
    both = nn(wide_ref[...], w2_ref[...])
    for o in range(2):
        hid = middle_ref[o].astype(F32)
        put_shifted(deep_ref, o, both[:, o * ch : (o + 1) * ch] * (1.0 - hid * hid))
    above_ref[...] = nn(wide_ref[:, :half], w2_ref[half:])
    below_ref[...] = nn(wide_ref[:, half:], w2_ref[:half])
    for p in range(2):
        both = nn(deep_ref[...], w1_ref[half * (1 - p) : half * (2 - p)])
        for o in range(2):
            row = 2 * p + o
            prior = precision_ref[...] * (state_ref[row] - background_ref[row])
            part_ref[row] = grad_ref[row] + both[:, o * ch : (o + 1) * ch] + prior
    copy.wait()


def outer_kernel(
    edge_ref,
    near_ref,
    far_ref,
    outside_ref,
    w1_ref,
    w2_ref,
    above_ref,
    below_ref,
    part_ref,
    out_hbm,
    wide_ref,
    deep_ref,
    out_ref,
    out_sems,
):
    rows, cols, ch = part_ref.shape
    half = 6 * ch
    for i in range(2):
        low, high = halo_row(edge_ref, near_ref, far_ref, i)
        put_shifted(wide_ref, i, low)
        put_shifted(wide_ref, 2 + i, high)
    for p, start_ref in enumerate((above_ref, below_ref)):
        both = start_ref[...] + nn(wide_ref[:, half * p : half * (p + 1)], w2_ref[half * p : half * (p + 1)])
        for o in range(2):
            hid = outside_ref[(2 * p + o) * cols : (2 * p + o + 1) * cols].astype(F32)
            act = both[:, o * ch : (o + 1) * ch] * (1.0 - hid * hid)
            put_shifted(deep_ref, 2 * p + o, in_grid(edge_ref, 3 * p + o, act))
    sent = []
    for p in range(2):
        both = nn(deep_ref[:, half * p : half * (p + 1)], w1_ref[half * p : half * (p + 1)])
        for o in range(2):
            row = 2 * p + o
            out_ref[row] = part_ref[row] + both[:, o * ch : (o + 1) * ch]
            sent.append(send(out_ref, out_hbm, out_sems, row, pl.ds(row, 1)))
    for copy in sent:
        copy.wait()


def swap_near(rows):
    count = lax.axis_size("dev")
    return lax.ppermute(rows, "dev", [(i, i ^ 1) for i in range(count)])


def swap_far(rows):
    count = lax.axis_size("dev")
    return lax.ppermute(rows, "dev", [(i, ((i + 1) ^ 1) - 1) for i in range(1, count - 1)])


def call(kernel, name, grant, places, out_shape, scratch, flops, *args):
    spaces = {"s": pltpu.SMEM, "v": pltpu.VMEM, "h": pltpu.HBM, "k": pltpu.HBM}
    places, made = places.split("-")
    staged = [pltpu.VMEM(o[0], o[1]) for o, p in zip(out_shape, made) if p == "h"]
    if set(made) & set("hk"):
        staged.append(pltpu.SemaphoreType.DMA((PIECES,)))
    fetched = [pltpu.VMEM(a.shape, a.dtype) for a, p in zip(args, places) if p == "h"]
    if set(places) & set("hk"):
        fetched.append(pltpu.SemaphoreType.DMA((PIECES,)))
    size = sum(a.size * a.dtype.itemsize for a in args)
    return pl.pallas_call(
        kernel,
        name=name,
        out_shape=[jax.ShapeDtypeStruct(s, d) for s, d in out_shape],
        in_specs=[pl.BlockSpec(memory_space=spaces[p]) for p in places],
        out_specs=[pl.BlockSpec(memory_space=spaces[p]) for p in made],
        scratch_shapes=[pltpu.VMEM(s, d) for s, d in scratch] + staged + fetched,
        compiler_params=pltpu.CompilerParams(vmem_limit_bytes=grant),
        cost_estimate=pl.CostEstimate(flops=flops, bytes_accessed=size, transcendentals=0),
    )(*args)


def per_device(
    state,
    background,
    back_precision,
    conv_first,
    bias_first,
    conv_second,
    sounding_tile,
    sounding_cells,
    cell_weights,
    observations,
    live_counts,
    layer_in,
    bias_in,
    layer_out,
    bias_out,
    error_precision,
):
    rows, cols, ch = state.shape
    devices = lax.axis_size("dev")
    slots = devices * CAP
    hid, channels = layer_out.shape
    width = channels + EXTRA
    edge = jnp.stack([lax.axis_index("dev").astype(jnp.int32), jnp.int32(devices)])
    (packed,) = call(
        pack_kernel,
        "pack",
        WIDE,
        "shhhh-h",
        [((slots, width), BF)],
        [((EXTRA, sounding_tile.shape[0]), F32)],
        2_000_000_000,
        live_counts,
        sounding_tile.T,
        sounding_cells.T,
        cell_weights.T,
        observations.T,
    )
    got = lax.all_to_all(packed.reshape(devices, CAP, width), "dev", split_axis=0, concat_axis=0, tiled=True)
    odd = edge[0] % 2
    near = swap_near(lax.dynamic_slice_in_dim(state, 2 * (1 - odd), 2).astype(BF))
    far = swap_far(lax.dynamic_slice_in_dim(state, 2 * odd, 2).astype(BF))
    out_pad, fold = call(
        fold_kernel,
        "fold",
        WIDE,
        "vv-vv",
        [((hid, width), BF), ((width, hid), BF)],
        [((width, hid), BF)],
        2_000_000_000,
        layer_out.T,
        error_precision,
    )
    bias_first, fold = lax.optimization_barrier((bias_first, fold))
    points = rows * cols
    pair = (12 * ch, 2 * ch)
    sums = [((cols, 2 * ch), F32), ((cols, 2 * ch), F32), ((rows, cols, ch), F32), (pair, BF), (pair, BF)]
    middle, above, below, part, w1, w2 = call(
        near_kernel,
        "near",
        NARROW,
        "vvvv-vvvvvv",
        [((2, cols, ch), BF)] + sums,
        [((cols, 12 * ch), BF), ((cols, 6 * ch), BF)],
        4_000_000_000,
        state,
        conv_first,
        bias_first[None],
        conv_second,
    )
    (kept,) = call(
        forecast_kernel,
        "forecast",
        MIDDLE,
        "svvvvvvvv-k",
        [((KEPT, ch), BF)],
        [((cols, 12 * ch), BF), ((cols, 12 * ch), BF), ((points, ch), BF), ((points, ch), BF)],
        2_000_000_000,
        edge,
        near,
        far,
        bias_first[None],
        w1,
        w2,
        above,
        below,
        part,
    )
    obs_grad, near, far = call(
        network_kernel,
        "network",
        SHARED,
        "svkhhhhh-vvv",
        [((points, ch), F32), ((points // 2, ch), BF), ((points // 2, ch), BF)],
        [((BLOCK, points), BF), ((points, ch), BF)],
        4_000_000_000,
        edge,
        got.reshape(slots, width),
        kept,
        layer_in,
        bias_in[None],
        out_pad,
        jnp.pad(bias_out, (0, width - channels))[None],
        fold,
    )
    far = swap_far(far.reshape(2, cols, ch))
    near = swap_near(near.reshape(2, cols, ch))
    above, below, part, w1, w2, outside = call(
        inner_kernel,
        "inner",
        MIDDLE,
        "vvvvvvvk-vvvvvv",
        sums + [((points, ch), BF)],
        [((cols, 12 * ch), BF), ((cols, 6 * ch), BF)],
        4_000_000_000,
        obs_grad.reshape(rows, cols, ch),
        middle,
        conv_first,
        conv_second,
        state,
        background,
        back_precision[None],
        kept,
    )
    (gradient,) = call(
        outer_kernel,
        "outer",
        NARROW,
        "svvvvvvvv-h",
        [((rows, cols, ch), F32)],
        [((cols, 12 * ch), BF), ((cols, 12 * ch), BF)],
        2_000_000_000,
        edge,
        near,
        far,
        outside,
        w1,
        w2,
        above,
        below,
        part,
    )
    return gradient


def solution(mesh):
    whole = P()
    split = P("dev", None)
    field = P("dev", None, None)
    return jax.shard_map(
        per_device,
        mesh=mesh,
        in_specs=(field, field) + (whole,) * 4 + (split,) * 4 + (P("dev"),) + (whole,) * 5,
        out_specs=field,
        check_vma=False,
    )
```
